32 devices in a mesh: ctx: 4 (over z), head: 8 (over y, x, core).
Axes of the slice: x: 2, y: 2, z: 4, core: 2. Of those that a mesh axis runs over, the one named last changes fastest.
Arguments:
- out_grad: bfloat16 [1536, 8192], P('ctx', 'head'), may hold values from -0.1796875 to 0.1796875
- conv_input: bfloat16 [1536, 8192], P('ctx', 'head'), may hold values from -0.119628906 to 0.119628906
- residues: float32 [16, 8192], P(None, 'head'), may hold values from -1.5 to 1.5
- decay_rate: float32 [16, 8192], P(None, 'head'), may hold values from 1e-05 to 0.033
- segments: int32 [1536], replicated, may hold values from 0 to 3, never falling along the last dimension, each value on 1 to 768 neighbouring positions
- w_in: bfloat16 [8192, 8192], P('head'), may hold values from -0.0625 to 0.0625
Outputs:
- d_input: bfloat16 [1536, 8192], P('ctx', 'head')
- filter_grad: float32 [16, 8192], P(None, 'head')
The draws below stay inside these ranges and needn't reach their ends.
Inputs may be any that keep to these rules, and one draw needn't show every extreme that they name: `segments`: document numbers never fall along the tokens; every document has 1 to 768 tokens and one has exactly 768.
All inputs are finite; a program needn't handle non-finite values.
Results may differ from the reference program's by a relative error of at most 0.0049.
Values may be sent and summed in bfloat16 or wider, within the bound.
A program may use at most 128 MiB of HBM per device.

```python
import math
import jax
import jax.numpy as jnp
import numpy as np
from jax import lax

D = 8192
MODES = 16
DOCS = 4
TOKENS = 1536


def level_of(own_key, shape, shards, least, top_value):
    def one(axis_at, parts):
        draws = jax.random.uniform(jax.random.fold_in(jax.random.fold_in(own_key, 6), axis_at), (parts,), jnp.float32, least / len(shards), top_value / len(shards))
        return jnp.repeat(jnp.exp(draws), shape[axis_at] // parts).reshape((-1,) + (1,) * (len(shape) - axis_at - 1))

    level = one(*shards[0])
    for cut in shards[1:]:
        level = level * one(*cut)
    return level


def length_profile(amount, total, most, slope):
    loads = [(1 << 20) // math.isqrt(rank ** slope) + 1 for rank in range(2, amount + 1)]
    spare, given = total - most - (amount - 1), [1] * (amount - 1)
    while spare > 0:
        free = [i for i in range(amount - 1) if given[i] < most]
        whole, remaining = sum([loads[i] for i in free]), spare
        for i in free:
            extra = min(most - given[i], max(1, remaining * loads[i] // whole), spare)
            given[i] = given[i] + extra
            spare = spare - extra
    return np.array([most] + given)


def uneven(key, count, total, most, skew):
    if count == 2:
        one = jax.random.randint(key, (), max(1, total - most), min(most, total - 1) + 1)
        return jnp.stack([one, total - one])
    lengths = jnp.asarray(length_profile(count, total, most, skew), jnp.int32)
    twos = (count - 1) // 2
    source_of, taker = lengths[1:1 + 2 * twos:2], lengths[2:2 + 2 * twos:2]
    room = jnp.minimum(source_of - 1, most - taker)
    moved = jax.random.randint(jax.random.fold_in(key, 1), (twos,), 0, 1 << 20) % (room + 1)
    lengths = lengths.at[1:1 + 2 * twos:2].set(source_of - moved).at[2:2 + 2 * twos:2].set(taker + moved)
    return lengths[jax.random.permutation(jax.random.fold_in(key, 2), count)]


def gaussian(rng, dims, scale, reach, shards=(), kind=jnp.bfloat16):
    array = scale * jax.random.normal(rng, dims, jnp.float32)
    if shards:
        array = array * level_of(rng, dims, shards, -0.22, 0.18)
    return jnp.clip(array, -reach, reach).astype(kind)


def setup_inputs(seed: int = 0) -> dict:
    seeds = jax.random.split(jax.random.key(seed), 7)
    out_grad = gaussian(seeds[0], (TOKENS, D), 0.03, 0.1796875, ((0, 4), (1, 8)))
    conv_input = gaussian(seeds[1], (TOKENS, D), 0.02, 0.119628906, ((0, 4), (1, 8)))
    residues = gaussian(seeds[2], (MODES, D), MODES ** -0.5, 1.5, ((1, 8),), jnp.float32)
    decay_rate = jnp.clip(jnp.exp(math.log(0.033) - 8.101678 * jax.random.uniform(seeds[3], (MODES, D), jnp.float32) ** level_of(seeds[3], (MODES, D), ((1, 8),), -0.2, 0.2)), 9.999999747378752e-06, 0.033)
    segments = jnp.searchsorted(jnp.cumsum(uneven(seeds[4], DOCS, TOKENS, TOKENS // 2, 0)), jnp.arange(TOKENS), side="right").astype(jnp.int32)
    w_in = gaussian(seeds[5], (D, D), D ** -0.5, 0.0625, ((0, 8),))
    return dict(out_grad=out_grad, conv_input=conv_input, residues=residues, decay_rate=decay_rate, segments=segments, w_in=w_in)


def reference(out_grad, conv_input, residues, decay_rate, segments, w_in):
    decay_factor = jnp.exp(-decay_rate)
    following = jnp.concatenate([segments[1:], jnp.full((1,), -1, jnp.int32)])
    link_flags = (segments == following).astype(jnp.float32)
    grad_rows = out_grad.astype(jnp.float32)
    input_rows = conv_input.astype(jnp.float32)

    def scan_step(state, scan_items):
        adjoint, filter_acc = state
        grad_row, input_row, link_flag = scan_items
        adjoint = grad_row[None, :] + link_flag * decay_factor * adjoint
        filter_acc = filter_acc + input_row[None, :] * adjoint
        conv_row = jnp.sum(residues * adjoint, axis=0)
        return (adjoint, filter_acc), conv_row

    zero_state = jnp.zeros(decay_factor.shape, jnp.float32)
    final_state, conv_grad = lax.scan(scan_step, (zero_state, zero_state), (grad_rows, input_rows, link_flags), reverse=True)
    filter_grad = final_state[1]
    conv_bf = conv_grad.astype(jnp.bfloat16)
    d_input = jnp.dot(conv_bf, w_in.T, preferred_element_type=jnp.float32).astype(jnp.bfloat16)
    return d_input, filter_grad
```

```python
import functools

import jax
import jax.numpy as jnp
from jax import lax
from jax.experimental import pallas as pl
from jax.experimental.pallas import tpu as pltpu
from jax.sharding import PartitionSpec as P

LANES = 128
VMEM = pl.BlockSpec(memory_space=pltpu.VMEM)
SMEM = pl.BlockSpec(memory_space=pltpu.SMEM)


def spread(src, dst, convert):
    rows, width = src.shape
    for tile in range(width // LANES):
        dst[pl.ds(tile * rows, rows), :] = convert(src[:, pl.ds(tile * LANES, LANES)])


def fold(src, dst, convert):
    rows, width = dst.shape
    for tile in range(width // LANES):
        dst[:, pl.ds(tile * LANES, LANES)] = convert(src[pl.ds(tile * rows, rows), :])


def wide(value):
    return value.astype(jnp.float32)


def fill_decay(rate_ref, mode_scr, decay_scr):
    modes = rate_ref.shape[0]
    subs = rate_ref.shape[1] // LANES
    spread(rate_ref, mode_scr, lambda v: jnp.exp(-v))
    for m in range(modes):
        decay_scr[0, m] = jnp.zeros((subs, LANES), jnp.float32)
        decay_scr[1, m] = mode_scr[pl.ds(m, subs, stride=modes), :]


def link_at(seg_ref, token):
    last = seg_ref.shape[0] - 1
    same = seg_ref[token] == seg_ref[jnp.minimum(token + 1, last)]
    return jnp.where(same, 1, 0)


def head_kernel(seg_ref, grad_ref, rate_ref, out_ref, grad_scr, mode_scr, decay_scr):
    rows, width = grad_ref.shape
    modes = rate_ref.shape[0]
    subs = width // LANES
    start = lax.axis_index("ctx") * rows
    spread(grad_ref, grad_scr, wide)
    fill_decay(rate_ref, mode_scr, decay_scr)

    def step(i, state):
        t = rows - 1 - i
        link = link_at(seg_ref, start + t)
        grad = grad_scr[pl.ds(t, subs, stride=rows), :]
        return tuple(grad + decay_scr[link, m] * state[m] for m in range(modes))

    zero = jnp.zeros((subs, LANES), jnp.float32)
    state = lax.fori_loop(0, rows, step, (zero,) * modes, unroll=8)
    for m in range(modes):
        out_ref[m] = state[m]


def main_kernel(
    seg_ref, grad_ref, input_ref, residue_ref, rate_ref, heads_ref,
    conv_ref, filter_ref,
    grad_scr, input_scr, conv_scr, mode_scr, through_scr, decay_scr, residue_scr, carry_scr,
):
    rows, width = grad_ref.shape
    modes = rate_ref.shape[0]
    subs = width // LANES
    place = lax.axis_index("ctx")
    count = heads_ref.shape[0]
    start = place * rows
    spread(grad_ref, grad_scr, wide)
    spread(input_ref, input_scr, wide)
    spread(residue_ref, mode_scr, lambda v: v)
    for m in range(modes):
        residue_scr[m] = mode_scr[pl.ds(m, subs, stride=modes), :]
    spread(rate_ref, mode_scr, lambda v: jnp.exp(-rows * v))
    for m in range(modes):
        through_scr[m] = mode_scr[pl.ds(m, subs, stride=modes), :]
    fill_decay(rate_ref, mode_scr, decay_scr)
    carry_scr[...] = jnp.zeros_like(carry_scr)
    last = seg_ref.shape[0] - 1

    def hop(i, carry):
        source = count - 1 - i
        same = seg_ref[source * rows] == seg_ref[jnp.minimum((source + 1) * rows, last)]
        linked = jnp.where(same, 1.0, 0.0)
        carry_scr[...] = heads_ref[source] + linked * through_scr[...] * carry_scr[...]
        return carry

    lax.fori_loop(0, count - 1 - place, hop, 0)

    def step(i, state):
        values, sums = state
        t = rows - 1 - i
        link = link_at(seg_ref, start + t)
        grad = grad_scr[pl.ds(t, subs, stride=rows), :]
        inputs = input_scr[pl.ds(t, subs, stride=rows), :]
        values = tuple(grad + decay_scr[link, m] * values[m] for m in range(modes))
        sums = tuple(sums[m] + inputs * values[m] for m in range(modes))
        parts = [residue_scr[m] * values[m] for m in range(modes)]
        while len(parts) > 1:
            parts = [a + b for a, b in zip(parts[::2], parts[1::2])]
        conv_scr[pl.ds(t, subs, stride=rows), :] = parts[0]
        return values, sums

    zero = jnp.zeros((subs, LANES), jnp.float32)
    values = tuple(carry_scr[m] for m in range(modes))
    _, sums = lax.fori_loop(0, rows, step, (values, (zero,) * modes), unroll=4)
    for m in range(modes):
        mode_scr[pl.ds(m, subs, stride=modes), :] = sums[m]
    fold(mode_scr, filter_ref, lambda v: v)
    fold(conv_scr, conv_ref, lambda v: v.astype(conv_ref.dtype))


def local(out_grad, conv_input, residues, decay_rate, segments, w_in):
    rows, width = out_grad.shape
    modes = residues.shape[0]
    subs = width // LANES
    f32 = jnp.float32
    tall = pltpu.VMEM((rows * subs, LANES), f32)
    flat = pltpu.VMEM((modes * subs, LANES), f32)
    packed = pltpu.VMEM((modes, subs, LANES), f32)
    decays = pltpu.VMEM((2, modes, subs, LANES), f32)
    params = pltpu.CompilerParams(vmem_limit_bytes=32 << 20)
    head = pl.pallas_call(
        head_kernel,
        out_shape=jax.ShapeDtypeStruct((modes, subs, LANES), f32),
        in_specs=[SMEM, VMEM, VMEM],
        out_specs=VMEM,
        scratch_shapes=[tall, flat, decays],
        compiler_params=params,
        name="head_state",
    )(segments, out_grad, decay_rate)
    heads = lax.all_gather(head, "ctx")
    conv_grad, partial = pl.pallas_call(
        main_kernel,
        out_shape=(
            jax.ShapeDtypeStruct((rows, width), jnp.bfloat16),
            jax.ShapeDtypeStruct((modes, width), f32),
        ),
        in_specs=[SMEM] + [VMEM] * 5,
        out_specs=(VMEM, VMEM),
        scratch_shapes=[tall, tall, tall, flat, packed, decays, packed, packed],
        compiler_params=params,
        name="adjoint_scan",
    )(segments, out_grad, conv_input, residues, decay_rate, heads)
    filter_grad = lax.psum(partial, "ctx")
    d_input = lax.dot_general(
        lax.all_gather(conv_grad, "head", axis=1, tiled=True),
        w_in,
        (((1,), (1,)), ((), ())),
        preferred_element_type=f32,
    )
    return (d_input.astype(jnp.bfloat16), filter_grad)


def solution(mesh):
    placed = (
        P("ctx", "head"),
        P("ctx", "head"),
        P(None, "head"),
        P(None, "head"),
        P(),
        P("head", None),
    )
    return jax.shard_map(
        local,
        mesh=mesh,
        in_specs=placed,
        out_specs=(P("ctx", "head"), P(None, "head")),
        check_vma=False,
    )
```

```python
import functools

import jax
import jax.numpy as jnp
from jax import lax
from jax.experimental import pallas as pl
from jax.experimental.pallas import tpu as pltpu
from jax.sharding import PartitionSpec as P

LANES = 128
VMEM = pl.BlockSpec(memory_space=pltpu.VMEM)
MESH = pl.DeviceIdType.MESH
SMEM = pl.BlockSpec(memory_space=pltpu.SMEM)


def spread(src, dst, convert):
    rows, width = src.shape
    for tile in range(width // LANES):
        dst[pl.ds(tile * rows, rows), :] = convert(src[:, pl.ds(tile * LANES, LANES)])


def fold(src, dst, convert):
    rows, width = dst.shape
    for tile in range(width // LANES):
        dst[:, pl.ds(tile * LANES, LANES)] = convert(src[pl.ds(tile * rows, rows), :])


def wide(value):
    return value.astype(jnp.float32)


def fill_decay(rate_ref, mode_scr, decay_scr):
    modes = rate_ref.shape[0]
    subs = rate_ref.shape[1] // LANES
    spread(rate_ref, mode_scr, lambda v: jnp.exp(-v))
    for m in range(modes):
        decay_scr[0, m] = jnp.zeros((subs, LANES), jnp.float32)
        decay_scr[1, m] = mode_scr[pl.ds(m, subs, stride=modes), :]


def link_at(seg_ref, token):
    last = seg_ref.shape[0] - 1
    same = seg_ref[token] == seg_ref[jnp.minimum(token + 1, last)]
    return jnp.where(same, 1, 0)


def head_kernel(seg_ref, grad_ref, rate_ref, out_ref, grad_scr, mode_scr, decay_scr):
    rows, width = grad_ref.shape
    modes = rate_ref.shape[0]
    subs = width // LANES
    start = lax.axis_index("ctx") * rows
    spread(grad_ref, grad_scr, wide)
    fill_decay(rate_ref, mode_scr, decay_scr)

    def step(i, state):
        t = rows - 1 - i
        link = link_at(seg_ref, start + t)
        grad = grad_scr[pl.ds(t, subs, stride=rows), :]
        return tuple(grad + decay_scr[link, m] * state[m] for m in range(modes))

    zero = jnp.zeros((subs, LANES), jnp.float32)
    state = lax.fori_loop(0, rows, step, (zero,) * modes, unroll=8)
    for m in range(modes):
        out_ref[m] = state[m]


def main_kernel(
    seg_ref, grad_ref, input_ref, residue_ref, rate_ref, heads_ref,
    conv_ref, filter_ref,
    grad_scr, input_scr, conv_scr, mode_scr, through_scr, decay_scr, residue_scr, carry_scr,
):
    rows, width = grad_ref.shape
    modes = rate_ref.shape[0]
    subs = width // LANES
    place = lax.axis_index("ctx")
    count = heads_ref.shape[0]
    start = place * rows
    spread(grad_ref, grad_scr, wide)
    spread(input_ref, input_scr, wide)
    spread(residue_ref, mode_scr, lambda v: v)
    for m in range(modes):
        residue_scr[m] = mode_scr[pl.ds(m, subs, stride=modes), :]
    spread(rate_ref, mode_scr, lambda v: jnp.exp(-rows * v))
    for m in range(modes):
        through_scr[m] = mode_scr[pl.ds(m, subs, stride=modes), :]
    fill_decay(rate_ref, mode_scr, decay_scr)
    carry_scr[...] = jnp.zeros_like(carry_scr)
    last = seg_ref.shape[0] - 1

    def hop(i, carry):
        source = count - 1 - i
        same = seg_ref[source * rows] == seg_ref[jnp.minimum((source + 1) * rows, last)]
        linked = jnp.where(same, 1.0, 0.0)
        carry_scr[...] = heads_ref[source - place] + linked * through_scr[...] * carry_scr[...]
        return carry

    lax.fori_loop(0, count - 1 - place, hop, 0)

    def step(i, state):
        values, sums = state
        t = rows - 1 - i
        link = link_at(seg_ref, start + t)
        grad = grad_scr[pl.ds(t, subs, stride=rows), :]
        inputs = input_scr[pl.ds(t, subs, stride=rows), :]
        values = tuple(grad + decay_scr[link, m] * values[m] for m in range(modes))
        sums = tuple(sums[m] + inputs * values[m] for m in range(modes))
        parts = [residue_scr[m] * values[m] for m in range(modes)]
        while len(parts) > 1:
            parts = [a + b for a, b in zip(parts[::2], parts[1::2])]
        conv_scr[pl.ds(t, subs, stride=rows), :] = parts[0]
        return values, sums

    zero = jnp.zeros((subs, LANES), jnp.float32)
    values = tuple(carry_scr[m] for m in range(modes))
    _, sums = lax.fori_loop(0, rows, step, (values, (zero,) * modes), unroll=4)
    for m in range(modes):
        mode_scr[pl.ds(m, subs, stride=modes), :] = sums[m]
    fold(mode_scr, filter_ref, lambda v: v)
    fold(conv_scr, conv_ref, lambda v: v.astype(conv_ref.dtype))


def exchange_kernel(head_ref, out_ref, send_sem, recv_sem):
    count = out_ref.shape[0]
    place = lax.axis_index("ctx")
    out_ref[...] = jnp.zeros_like(out_ref)
    barrier = pltpu.get_barrier_semaphore()
    for d in range(1, count):
        other = lax.rem(place + d, count)
        pl.semaphore_signal(barrier, inc=1, device_id={"ctx": other}, device_id_type=MESH)
    pl.semaphore_wait(barrier, count - 1)
    copies = []
    for d in range(1, count):
        other = jnp.maximum(place - d, 0)
        copies.append(pltpu.make_async_remote_copy(
            src_ref=head_ref,
            dst_ref=out_ref.at[d],
            send_sem=send_sem.at[d],
            recv_sem=recv_sem.at[d],
            device_id={"ctx": other},
            device_id_type=MESH,
        ))
    for d in range(1, count):
        pl.when(place >= d)(copies[d - 1].start)
    for d in range(1, count):
        pl.when(place >= d)(copies[d - 1].wait_send)
        pl.when(place + d < count)(copies[d - 1].wait_recv)


def gather_kernel(
    conv_ref, w_ref, part_ref, out_ref, filter_ref,
    blocks, weights, total, parts,
    send_sem, recv_sem, weight_sem, part_send, part_recv,
):
    rows, width = conv_ref.shape
    half = rows // 2
    count = parts.shape[0]
    place = lax.axis_index("ctx")
    me = lax.axis_index("head")
    core = lax.rem(me, 2)
    east = lax.rem(me // 2, 2)
    north = me // 4
    steps = {1: 1 - 2 * core, 2: 2 - 4 * east, 4: 4 - 8 * north}

    def apart(k):
        return me + sum(steps[bit] for bit in steps if k & bit)

    loads = []
    for k in range(8):
        loads.append(pltpu.make_async_copy(
            w_ref.at[:, pl.ds(pl.multiple_of(apart(k) * width, LANES), width)],
            weights.at[k],
            weight_sem.at[k],
        ))
        loads[k].start()

    barrier = pltpu.get_barrier_semaphore()
    for bit in steps:
        pl.semaphore_signal(barrier, inc=1, device_id={"head": apart(bit)}, device_id_type=MESH)
    for d in range(1, count):
        other = lax.rem(place + d, count)
        pl.semaphore_signal(barrier, inc=1, device_id={"ctx": other}, device_id_type=MESH)
    pl.semaphore_wait(barrier, 3 + count - 1)

    def piece(k, h):
        if k == 0:
            return conv_ref.at[pl.ds(h * half, half)]
        return blocks.at[k - 1, pl.ds(h * half, half)]

    sent = {}

    def send(k, h, bit):
        copy = pltpu.make_async_remote_copy(
            src_ref=piece(k, h),
            dst_ref=piece(k ^ bit, h),
            send_sem=send_sem.at[(k ^ bit) - 1, h],
            recv_sem=recv_sem.at[(k ^ bit) - 1, h],
            device_id={"head": apart(bit)},
            device_id_type=MESH,
        )
        copy.start()
        sent[k ^ bit, h] = copy

    def multiply(k, first, size):
        def tile(n, carry):
            columns = pl.ds(pl.multiple_of(n * 256, 256), 256)
            source = conv_ref if k == 0 else blocks.at[k - 1]
            product = lax.dot_general(
                source[pl.ds(first, size), :],
                weights[k, columns, :],
                (((1,), (1,)), ((), ())),
                preferred_element_type=jnp.float32,
            )
            if k == 0:
                total[pl.ds(first, size), columns] = product
            else:
                total[pl.ds(first, size), columns] += product
            return carry

        lax.fori_loop(0, total.shape[1] // 256, tile, 0)

    send(0, 0, 2)
    send(0, 1, 4)
    send(0, 1, 2)
    send(0, 0, 4)
    send(0, 0, 1)
    send(0, 1, 1)
    sums = []
    for d in range(1, count):
        other = lax.rem(place + d, count)
        sums.append(pltpu.make_async_remote_copy(
            src_ref=part_ref,
            dst_ref=parts.at[count - d],
            send_sem=part_send.at[d],
            recv_sem=part_recv.at[count - d],
            device_id={"ctx": other},
            device_id_type=MESH,
        ))
        sums[-1].start()
    parts[0] = part_ref[...]
    loads[0].wait()
    multiply(0, 0, rows)
    sent[1, 0].wait_recv()
    sent[1, 1].wait_recv()
    loads[1].wait()
    multiply(1, 0, rows)
    sent[2, 0].wait_recv()
    send(2, 0, 4)
    send(2, 0, 1)
    sent[4, 1].wait_recv()
    send(4, 1, 2)
    send(4, 1, 1)
    for k in (2, 3, 4, 5):
        loads[k].wait()
    multiply(2, 0, half)
    multiply(4, half, half)
    sent[3, 0].wait_recv()
    multiply(3, 0, half)
    sent[5, 1].wait_recv()
    multiply(5, half, half)
    for copy in sums:
        copy.wait()
    value = parts[lax.rem(count - place, count)]
    for z in range(1, count):
        value = value + parts[lax.rem(z + count - place, count)]
    filter_ref[...] = value
    sent[2, 1].wait_recv()
    send(2, 1, 1)
    sent[4, 0].wait_recv()
    send(4, 0, 1)
    multiply(2, half, half)
    multiply(4, 0, half)
    sent[3, 1].wait_recv()
    multiply(3, half, half)
    sent[5, 0].wait_recv()
    multiply(5, 0, half)
    sent[6, 0].wait_recv()
    send(6, 0, 1)
    sent[6, 1].wait_recv()
    send(6, 1, 1)
    loads[6].wait()
    multiply(6, 0, rows)
    sent[7, 0].wait_recv()
    sent[7, 1].wait_recv()
    loads[7].wait()
    multiply(7, 0, rows)
    for copy in sent.values():
        copy.wait_send()
    out_ref[...] = total[...].astype(out_ref.dtype)


def exchange(head):
    count = lax.axis_size("ctx")
    return pl.pallas_call(
        exchange_kernel,
        out_shape=jax.ShapeDtypeStruct((count,) + head.shape, head.dtype),
        in_specs=[VMEM],
        out_specs=VMEM,
        scratch_shapes=[pltpu.SemaphoreType.DMA((count,))] * 2,
        compiler_params=pltpu.CompilerParams(collective_id=1, has_side_effects=True),
        name="head_exchange",
    )(head)


def gather_multiply(conv_grad, w_in, partial):
    rows, width = conv_grad.shape
    features = w_in.shape[0]
    count = lax.axis_size("ctx")
    dma = pltpu.SemaphoreType.DMA
    return pl.pallas_call(
        gather_kernel,
        out_shape=(
            jax.ShapeDtypeStruct((rows, features), jnp.bfloat16),
            jax.ShapeDtypeStruct(partial.shape, partial.dtype),
        ),
        in_specs=[VMEM, pl.BlockSpec(memory_space=pl.ANY), VMEM],
        out_specs=(VMEM, VMEM),
        scratch_shapes=[
            pltpu.VMEM((7, rows, width), jnp.bfloat16),
            pltpu.VMEM((8, features, width), jnp.bfloat16),
            pltpu.VMEM((rows, features), jnp.float32),
            pltpu.VMEM((count,) + partial.shape, partial.dtype),
            dma((7, 2)), dma((7, 2)), dma((8,)), dma((count,)), dma((count,)),
        ],
        compiler_params=pltpu.CompilerParams(
            collective_id=2, has_side_effects=True, vmem_limit_bytes=44 << 20
        ),
        cost_estimate=pl.CostEstimate(
            flops=16 * rows * width * features,
            bytes_accessed=16 * features * width,
            transcendentals=0,
        ),
        name="gather_multiply",
    )(conv_grad, w_in, partial)


def local(out_grad, conv_input, residues, decay_rate, segments, w_in):
    rows, width = out_grad.shape
    modes = residues.shape[0]
    subs = width // LANES
    f32 = jnp.float32
    tall = pltpu.VMEM((rows * subs, LANES), f32)
    flat = pltpu.VMEM((modes * subs, LANES), f32)
    packed = pltpu.VMEM((modes, subs, LANES), f32)
    decays = pltpu.VMEM((2, modes, subs, LANES), f32)
    params = pltpu.CompilerParams(vmem_limit_bytes=32 << 20)
    head = pl.pallas_call(
        head_kernel,
        out_shape=jax.ShapeDtypeStruct((modes, subs, LANES), f32),
        in_specs=[SMEM, VMEM, VMEM],
        out_specs=VMEM,
        scratch_shapes=[tall, flat, decays],
        compiler_params=params,
        name="head_state",
    )(segments, out_grad, decay_rate)
    heads = exchange(head)
    conv_grad, partial = pl.pallas_call(
        main_kernel,
        out_shape=(
            jax.ShapeDtypeStruct((rows, width), jnp.bfloat16),
            jax.ShapeDtypeStruct((modes, width), f32),
        ),
        in_specs=[SMEM] + [VMEM] * 5,
        out_specs=(VMEM, VMEM),
        scratch_shapes=[tall, tall, tall, flat, packed, decays, packed, packed],
        compiler_params=params,
        name="adjoint_scan",
    )(segments, out_grad, conv_input, residues, decay_rate, heads)
    if lax.axis_size("head") == 8:
        return gather_multiply(conv_grad, w_in, partial)
    filter_grad = lax.psum(partial, "ctx")
    d_input = lax.dot_general(
        lax.all_gather(conv_grad, "head", axis=1, tiled=True),
        w_in,
        (((1,), (1,)), ((), ())),
        preferred_element_type=f32,
    )
    return (d_input.astype(jnp.bfloat16), filter_grad)


def solution(mesh):
    placed = (
        P("ctx", "head"),
        P("ctx", "head"),
        P(None, "head"),
        P(None, "head"),
        P(),
        P("head", None),
    )
    return jax.shard_map(
        local,
        mesh=mesh,
        in_specs=placed,
        out_specs=(P("ctx", "head"), P(None, "head")),
        check_vma=False,
    )
```

```python
import functools

import jax
import jax.numpy as jnp
from jax import lax
from jax.experimental import pallas as pl
from jax.experimental.pallas import tpu as pltpu
from jax.sharding import PartitionSpec as P

LANES = 128
VMEM = pl.BlockSpec(memory_space=pltpu.VMEM)
MESH = pl.DeviceIdType.MESH
SMEM = pl.BlockSpec(memory_space=pltpu.SMEM)


def spread(src, dst, convert):
    rows, width = src.shape
    for tile in range(width // LANES):
        dst[pl.ds(tile * rows, rows), :] = convert(src[:, pl.ds(tile * LANES, LANES)])


def fold(src, dst, convert):
    rows, width = dst.shape
    for tile in range(width // LANES):
        dst[:, pl.ds(tile * LANES, LANES)] = convert(src[pl.ds(tile * rows, rows), :])


def wide(value):
    return value.astype(jnp.float32)


def fill_decay(rate_ref, mode_scr, decay_scr):
    modes = rate_ref.shape[0]
    subs = rate_ref.shape[1] // LANES
    spread(rate_ref, mode_scr, lambda v: jnp.exp(-v))
    for m in range(modes):
        decay_scr[0, m] = jnp.zeros((subs, LANES), jnp.float32)
        decay_scr[1, m] = mode_scr[pl.ds(m, subs, stride=modes), :]


def link_at(seg_ref, token):
    last = seg_ref.shape[0] - 1
    same = seg_ref[token] == seg_ref[jnp.minimum(token + 1, last)]
    return jnp.where(same, 1, 0)


def head_kernel(seg_ref, grad_ref, rate_ref, out_ref, grad_scr, mode_scr, decay_scr):
    rows, width = grad_ref.shape
    modes = rate_ref.shape[0]
    subs = width // LANES
    start = lax.axis_index("ctx") * rows
    spread(grad_ref, grad_scr, wide)
    fill_decay(rate_ref, mode_scr, decay_scr)

    def step(i, state):
        t = rows - 1 - i
        link = link_at(seg_ref, start + t)
        grad = grad_scr[pl.ds(t, subs, stride=rows), :]
        return tuple(grad + decay_scr[link, m] * state[m] for m in range(modes))

    zero = jnp.zeros((subs, LANES), jnp.float32)
    state = lax.fori_loop(0, rows, step, (zero,) * modes, unroll=8)
    for m in range(modes):
        out_ref[m] = state[m]


def main_kernel(
    seg_ref, grad_ref, input_ref, residue_ref, rate_ref, heads_ref,
    conv_ref, filter_ref,
    grad_scr, input_scr, conv_scr, mode_scr, through_scr, decay_scr, residue_scr, carry_scr,
):
    rows, width = grad_ref.shape
    modes = rate_ref.shape[0]
    subs = width // LANES
    place = lax.axis_index("ctx")
    count = heads_ref.shape[0]
    start = place * rows
    spread(grad_ref, grad_scr, wide)
    spread(input_ref, input_scr, wide)
    spread(residue_ref, mode_scr, lambda v: v)
    for m in range(modes):
        residue_scr[m] = mode_scr[pl.ds(m, subs, stride=modes), :]
    spread(rate_ref, mode_scr, lambda v: jnp.exp(-rows * v))
    for m in range(modes):
        through_scr[m] = mode_scr[pl.ds(m, subs, stride=modes), :]
    fill_decay(rate_ref, mode_scr, decay_scr)
    carry_scr[...] = jnp.zeros_like(carry_scr)
    last = seg_ref.shape[0] - 1

    def hop(i, carry):
        source = count - 1 - i
        same = seg_ref[source * rows] == seg_ref[jnp.minimum((source + 1) * rows, last)]
        linked = jnp.where(same, 1.0, 0.0)
        carry_scr[...] = heads_ref[source - place] + linked * through_scr[...] * carry_scr[...]
        return carry

    lax.fori_loop(0, count - 1 - place, hop, 0)

    def step(i, state):
        values, sums = state
        t = rows - 1 - i
        link = link_at(seg_ref, start + t)
        grad = grad_scr[pl.ds(t, subs, stride=rows), :]
        inputs = input_scr[pl.ds(t, subs, stride=rows), :]
        values = tuple(grad + decay_scr[link, m] * values[m] for m in range(modes))
        sums = tuple(sums[m] + inputs * values[m] for m in range(modes))
        parts = [residue_scr[m] * values[m] for m in range(modes)]
        while len(parts) > 1:
            parts = [a + b for a, b in zip(parts[::2], parts[1::2])]
        conv_scr[pl.ds(t, subs, stride=rows), :] = parts[0]
        return values, sums

    zero = jnp.zeros((subs, LANES), jnp.float32)
    values = tuple(carry_scr[m] for m in range(modes))
    _, sums = lax.fori_loop(0, rows, step, (values, (zero,) * modes), unroll=4)
    for m in range(modes):
        mode_scr[pl.ds(m, subs, stride=modes), :] = sums[m]
    fold(mode_scr, filter_ref, lambda v: v)
    fold(conv_scr, conv_ref, lambda v: v.astype(conv_ref.dtype))


def exchange_kernel(head_ref, out_ref, send_sem, recv_sem):
    count = out_ref.shape[0]
    place = lax.axis_index("ctx")
    out_ref[...] = jnp.zeros_like(out_ref)
    barrier = pltpu.get_barrier_semaphore()
    for d in range(1, count):
        other = lax.rem(place + d, count)
        pl.semaphore_signal(barrier, inc=1, device_id={"ctx": other}, device_id_type=MESH)
    pl.semaphore_wait(barrier, count - 1)
    copies = []
    for d in range(1, count):
        other = jnp.maximum(place - d, 0)
        copies.append(pltpu.make_async_remote_copy(
            src_ref=head_ref,
            dst_ref=out_ref.at[d],
            send_sem=send_sem.at[d],
            recv_sem=recv_sem.at[d],
            device_id={"ctx": other},
            device_id_type=MESH,
        ))
    for d in range(1, count):
        pl.when(place >= d)(copies[d - 1].start)
    for d in range(1, count):
        pl.when(place >= d)(copies[d - 1].wait_send)
        pl.when(place + d < count)(copies[d - 1].wait_recv)


def fused_kernel(
    seg_ref, grad_hbm, input_hbm, residue_hbm, rate_hbm, w_ref, out_ref, filter_ref,
    grad_ref, input_ref, residue_ref, rate_ref, conv_ref, part_ref, head_ref, heads_ref,
    grad_scr, input_scr, conv_scr, mode_scr, through_scr, decay_scr, residue_scr, carry_scr,
    blocks, weights, total, parts,
    send_sem, recv_sem, weight_sem, part_send, part_recv, head_send, head_recv, load_sem,
):
    rows, width = conv_ref.shape
    modes = rate_ref.shape[0]
    subs = width // LANES
    half = rows // 2
    count = parts.shape[0]
    place = lax.axis_index("ctx")
    me = lax.axis_index("head")
    core = lax.rem(me, 2)
    east = lax.rem(me // 2, 2)
    north = me // 4
    steps = {1: 1 - 2 * core, 2: 2 - 4 * east, 4: 4 - 8 * north}

    def apart(k):
        return me + sum(steps[bit] for bit in steps if k & bit)

    operands = []
    for i, (src, dst) in enumerate((
        (grad_hbm, grad_ref), (rate_hbm, rate_ref),
        (input_hbm, input_ref), (residue_hbm, residue_ref),
    )):
        operands.append(pltpu.make_async_copy(src, dst, load_sem.at[i]))
        operands[i].start()
    loads = []
    for k in range(8):
        loads.append(pltpu.make_async_copy(
            w_ref.at[:, pl.ds(pl.multiple_of(apart(k) * width, LANES), width)],
            weights.at[k],
            weight_sem.at[k],
        ))
        loads[k].start()

    barrier = pltpu.get_barrier_semaphore()
    for bit in steps:
        pl.semaphore_signal(barrier, inc=1, device_id={"head": apart(bit)}, device_id_type=MESH)
    for d in range(1, count):
        other = lax.rem(place + d, count)
        pl.semaphore_signal(barrier, inc=1, device_id={"ctx": other}, device_id_type=MESH)

    start = place * rows
    zero = jnp.zeros((subs, LANES), jnp.float32)
    operands[0].wait()
    spread(grad_ref, grad_scr, wide)
    operands[1].wait()
    fill_decay(rate_ref, mode_scr, decay_scr)

    def head_step(i, state):
        t = rows - 1 - i
        link = link_at(seg_ref, start + t)
        grad = grad_scr[pl.ds(t, subs, stride=rows), :]
        return tuple(grad + decay_scr[link, m] * state[m] for m in range(modes))

    state = lax.fori_loop(0, rows, head_step, (zero,) * modes, unroll=8)
    for m in range(modes):
        head_ref[m] = state[m]
    pl.semaphore_wait(barrier, 3 + count - 1)
    copies = []
    for d in range(1, count):
        copies.append(pltpu.make_async_remote_copy(
            src_ref=head_ref,
            dst_ref=heads_ref.at[d],
            send_sem=head_send.at[d],
            recv_sem=head_recv.at[d],
            device_id={"ctx": jnp.maximum(place - d, 0)},
            device_id_type=MESH,
        ))
    for d in range(1, count):
        pl.when(place >= d)(copies[d - 1].start)

    spread(rate_ref, mode_scr, lambda v: jnp.exp(-rows * v))
    for m in range(modes):
        through_scr[m] = mode_scr[pl.ds(m, subs, stride=modes), :]
    operands[2].wait()
    spread(input_ref, input_scr, wide)
    operands[3].wait()
    spread(residue_ref, mode_scr, lambda v: v)
    for m in range(modes):
        residue_scr[m] = mode_scr[pl.ds(m, subs, stride=modes), :]
    carry_scr[...] = jnp.zeros_like(carry_scr)
    last = seg_ref.shape[0] - 1

    def hop(d):
        copies[d - 1].wait_recv()
        source = place + d
        same = seg_ref[source * rows] == seg_ref[jnp.minimum((source + 1) * rows, last)]
        linked = jnp.where(same, 1.0, 0.0)
        carry_scr[...] = heads_ref[d] + linked * through_scr[...] * carry_scr[...]

    for d in range(count - 1, 0, -1):
        pl.when(place + d < count)(functools.partial(hop, d))

    def step(i, state):
        values, sums = state
        t = rows - 1 - i
        link = link_at(seg_ref, start + t)
        grad = grad_scr[pl.ds(t, subs, stride=rows), :]
        inputs = input_scr[pl.ds(t, subs, stride=rows), :]
        values = tuple(grad + decay_scr[link, m] * values[m] for m in range(modes))
        sums = tuple(sums[m] + inputs * values[m] for m in range(modes))
        terms = [residue_scr[m] * values[m] for m in range(modes)]
        while len(terms) > 1:
            terms = [a + b for a, b in zip(terms[::2], terms[1::2])]
        conv_scr[pl.ds(t, subs, stride=rows), :] = terms[0]
        return values, sums

    def round_rows(first):
        for tile in range(subs):
            conv_ref[pl.ds(first, half), pl.ds(tile * LANES, LANES)] = conv_scr[
                pl.ds(tile * rows + first, half), :
            ].astype(conv_ref.dtype)

    def piece(k, h):
        if k == 0:
            return conv_ref.at[pl.ds(h * half, half)]
        return blocks.at[k - 1, pl.ds(h * half, half)]

    sent = {}

    def send(k, h, bit):
        copy = pltpu.make_async_remote_copy(
            src_ref=piece(k, h),
            dst_ref=piece(k ^ bit, h),
            send_sem=send_sem.at[(k ^ bit) - 1, h],
            recv_sem=recv_sem.at[(k ^ bit) - 1, h],
            device_id={"head": apart(bit)},
            device_id_type=MESH,
        )
        copy.start()
        sent[k ^ bit, h] = copy

    def multiply(k, first, size):
        def tile(n, carry):
            columns = pl.ds(pl.multiple_of(n * 256, 256), 256)
            source = conv_ref if k == 0 else blocks.at[k - 1]
            product = lax.dot_general(
                source[pl.ds(first, size), :],
                weights[k, columns, :],
                (((1,), (1,)), ((), ())),
                preferred_element_type=jnp.float32,
            )
            if k == 0:
                total[pl.ds(first, size), columns] = product
            else:
                total[pl.ds(first, size), columns] += product
            return carry

        lax.fori_loop(0, total.shape[1] // 256, tile, 0)

    state = (tuple(carry_scr[m] for m in range(modes)), (zero,) * modes)
    state = lax.fori_loop(0, half, step, state, unroll=4)
    round_rows(half)
    send(0, 1, 2)
    send(0, 1, 4)
    send(0, 1, 1)
    _, state = lax.fori_loop(half, rows, step, state, unroll=4)
    round_rows(0)
    send(0, 0, 2)
    send(0, 0, 4)
    send(0, 0, 1)
    for m in range(modes):
        mode_scr[pl.ds(m, subs, stride=modes), :] = state[m]
    fold(mode_scr, part_ref, lambda v: v)
    sums = []
    for d in range(1, count):
        other = lax.rem(place + d, count)
        sums.append(pltpu.make_async_remote_copy(
            src_ref=part_ref,
            dst_ref=parts.at[count - d],
            send_sem=part_send.at[d],
            recv_sem=part_recv.at[count - d],
            device_id={"ctx": other},
            device_id_type=MESH,
        ))
        sums[-1].start()
    parts[0] = part_ref[...]
    loads[0].wait()
    multiply(0, 0, rows)
    sent[4, 1].wait_recv()
    send(4, 1, 2)
    send(4, 1, 1)
    sent[2, 1].wait_recv()
    send(2, 1, 1)
    for k in (1, 2, 3, 4, 5):
        loads[k].wait()
    sent[1, 1].wait_recv()
    sent[1, 0].wait_recv()
    multiply(1, 0, rows)
    multiply(4, half, half)
    multiply(2, half, half)
    sent[5, 1].wait_recv()
    multiply(5, half, half)
    sent[3, 1].wait_recv()
    multiply(3, half, half)
    for copy in sums:
        copy.wait()
    value = parts[lax.rem(count - place, count)]
    for z in range(1, count):
        value = value + parts[lax.rem(z + count - place, count)]
    filter_ref[...] = value
    sent[2, 0].wait_recv()
    send(2, 0, 4)
    send(2, 0, 1)
    sent[4, 0].wait_recv()
    send(4, 0, 1)
    multiply(2, 0, half)
    multiply(4, 0, half)
    sent[3, 0].wait_recv()
    multiply(3, 0, half)
    sent[5, 0].wait_recv()
    multiply(5, 0, half)
    loads[6].wait()
    loads[7].wait()
    for h in (1, 0):
        sent[6, h].wait_recv()
        send(6, h, 1)
        multiply(6, h * half, half)
    for h in (1, 0):
        sent[7, h].wait_recv()
        multiply(7, h * half, half)
    for d in range(1, count):
        pl.when(place >= d)(copies[d - 1].wait_send)
    for copy in sent.values():
        copy.wait_send()
    out_ref[...] = total[...].astype(out_ref.dtype)


def exchange(head):
    count = lax.axis_size("ctx")
    return pl.pallas_call(
        exchange_kernel,
        out_shape=jax.ShapeDtypeStruct((count,) + head.shape, head.dtype),
        in_specs=[VMEM],
        out_specs=VMEM,
        scratch_shapes=[pltpu.SemaphoreType.DMA((count,))] * 2,
        compiler_params=pltpu.CompilerParams(collective_id=1, has_side_effects=True),
        name="head_exchange",
    )(head)


def fused(out_grad, conv_input, residues, decay_rate, segments, w_in):
    rows, width = out_grad.shape
    modes = residues.shape[0]
    features = w_in.shape[0]
    subs = width // LANES
    count = lax.axis_size("ctx")
    dma = pltpu.SemaphoreType.DMA
    f32, bf16 = jnp.float32, jnp.bfloat16
    tall = pltpu.VMEM((rows * subs, LANES), f32)
    packed = pltpu.VMEM((modes, subs, LANES), f32)
    block = pltpu.VMEM((rows, width), bf16)
    small = pltpu.VMEM((modes, width), f32)
    return pl.pallas_call(
        fused_kernel,
        out_shape=(
            jax.ShapeDtypeStruct((rows, features), bf16),
            jax.ShapeDtypeStruct((modes, width), f32),
        ),
        in_specs=[SMEM] + [pl.BlockSpec(memory_space=pl.ANY)] * 5,
        out_specs=(VMEM, VMEM),
        scratch_shapes=[
            block, block, small, small, block, small, packed,
            pltpu.VMEM((count, modes, subs, LANES), f32),
            tall, tall, tall,
            pltpu.VMEM((modes * subs, LANES), f32),
            packed,
            pltpu.VMEM((2, modes, subs, LANES), f32),
            packed, packed,
            pltpu.VMEM((7, rows, width), bf16),
            pltpu.VMEM((8, features, width), bf16),
            pltpu.VMEM((rows, features), f32),
            pltpu.VMEM((count, modes, width), f32),
            dma((7, 2)), dma((7, 2)), dma((8,)), dma((count,)), dma((count,)),
            dma((count,)), dma((count,)), dma((4,)),
        ],
        compiler_params=pltpu.CompilerParams(
            collective_id=2, has_side_effects=True, vmem_limit_bytes=56 << 20
        ),
        cost_estimate=pl.CostEstimate(
            flops=16 * rows * width * features,
            bytes_accessed=16 * features * width,
            transcendentals=0,
        ),
        name="fused_backward",
    )(segments, out_grad, conv_input, residues, decay_rate, w_in)


def local(out_grad, conv_input, residues, decay_rate, segments, w_in):
    if lax.axis_size("head") == 8:
        return fused(out_grad, conv_input, residues, decay_rate, segments, w_in)
    rows, width = out_grad.shape
    modes = residues.shape[0]
    subs = width // LANES
    f32 = jnp.float32
    tall = pltpu.VMEM((rows * subs, LANES), f32)
    flat = pltpu.VMEM((modes * subs, LANES), f32)
    packed = pltpu.VMEM((modes, subs, LANES), f32)
    decays = pltpu.VMEM((2, modes, subs, LANES), f32)
    params = pltpu.CompilerParams(vmem_limit_bytes=32 << 20)
    head = pl.pallas_call(
        head_kernel,
        out_shape=jax.ShapeDtypeStruct((modes, subs, LANES), f32),
        in_specs=[SMEM, VMEM, VMEM],
        out_specs=VMEM,
        scratch_shapes=[tall, flat, decays],
        compiler_params=params,
        name="head_state",
    )(segments, out_grad, decay_rate)
    heads = exchange(head)
    conv_grad, partial = pl.pallas_call(
        main_kernel,
        out_shape=(
            jax.ShapeDtypeStruct((rows, width), jnp.bfloat16),
            jax.ShapeDtypeStruct((modes, width), f32),
        ),
        in_specs=[SMEM] + [VMEM] * 5,
        out_specs=(VMEM, VMEM),
        scratch_shapes=[tall, tall, tall, flat, packed, decays, packed, packed],
        compiler_params=params,
        name="adjoint_scan",
    )(segments, out_grad, conv_input, residues, decay_rate, heads)
    filter_grad = lax.psum(partial, "ctx")
    d_input = lax.dot_general(
        lax.all_gather(conv_grad, "head", axis=1, tiled=True),
        w_in,
        (((1,), (1,)), ((), ())),
        preferred_element_type=f32,
    )
    return (d_input.astype(jnp.bfloat16), filter_grad)


def solution(mesh):
    placed = (
        P("ctx", "head"),
        P("ctx", "head"),
        P(None, "head"),
        P(None, "head"),
        P(),
        P("head", None),
    )
    return jax.shard_map(
        local,
        mesh=mesh,
        in_specs=placed,
        out_specs=(P("ctx", "head"), P(None, "head")),
        check_vma=False,
    )
```

```python
import functools

import jax
import jax.numpy as jnp
from jax import lax
from jax.experimental import pallas as pl
from jax.experimental.pallas import tpu as pltpu
from jax.sharding import PartitionSpec as P

LANES = 128
VMEM = pl.BlockSpec(memory_space=pltpu.VMEM)
MESH = pl.DeviceIdType.MESH
SMEM = pl.BlockSpec(memory_space=pltpu.SMEM)


def spread(src, dst, convert):
    rows, width = src.shape
    for tile in range(width // LANES):
        dst[pl.ds(tile * rows, rows), :] = convert(src[:, pl.ds(tile * LANES, LANES)])


def fold(src, dst, convert):
    rows, width = dst.shape
    for tile in range(width // LANES):
        dst[:, pl.ds(tile * LANES, LANES)] = convert(src[pl.ds(tile * rows, rows), :])


def wide(value):
    return value.astype(jnp.float32)


def fill_decay(rate_ref, mode_scr, decay_scr):
    modes = rate_ref.shape[0]
    subs = rate_ref.shape[1] // LANES
    spread(rate_ref, mode_scr, lambda v: jnp.exp(-v))
    for m in range(modes):
        decay_scr[0, m] = jnp.zeros((subs, LANES), jnp.float32)
        decay_scr[1, m] = mode_scr[pl.ds(m, subs, stride=modes), :]


def link_at(seg_ref, token):
    last = seg_ref.shape[0] - 1
    same = seg_ref[token] == seg_ref[jnp.minimum(token + 1, last)]
    return jnp.where(same, 1, 0)


def head_kernel(seg_ref, grad_ref, rate_ref, out_ref, grad_scr, mode_scr, decay_scr):
    rows, width = grad_ref.shape
    modes = rate_ref.shape[0]
    subs = width // LANES
    start = lax.axis_index("ctx") * rows
    spread(grad_ref, grad_scr, wide)
    fill_decay(rate_ref, mode_scr, decay_scr)

    def step(i, state):
        t = rows - 1 - i
        link = link_at(seg_ref, start + t)
        grad = grad_scr[pl.ds(t, subs, stride=rows), :]
        return tuple(grad + decay_scr[link, m] * state[m] for m in range(modes))

    zero = jnp.zeros((subs, LANES), jnp.float32)
    state = lax.fori_loop(0, rows, step, (zero,) * modes, unroll=8)
    for m in range(modes):
        out_ref[m] = state[m]


def main_kernel(
    seg_ref, grad_ref, input_ref, residue_ref, rate_ref, heads_ref,
    conv_ref, filter_ref,
    grad_scr, input_scr, conv_scr, mode_scr, through_scr, decay_scr, residue_scr, carry_scr,
):
    rows, width = grad_ref.shape
    modes = rate_ref.shape[0]
    subs = width // LANES
    place = lax.axis_index("ctx")
    count = heads_ref.shape[0]
    start = place * rows
    spread(grad_ref, grad_scr, wide)
    spread(input_ref, input_scr, wide)
    spread(residue_ref, mode_scr, lambda v: v)
    for m in range(modes):
        residue_scr[m] = mode_scr[pl.ds(m, subs, stride=modes), :]
    spread(rate_ref, mode_scr, lambda v: jnp.exp(-rows * v))
    for m in range(modes):
        through_scr[m] = mode_scr[pl.ds(m, subs, stride=modes), :]
    fill_decay(rate_ref, mode_scr, decay_scr)
    carry_scr[...] = jnp.zeros_like(carry_scr)
    last = seg_ref.shape[0] - 1

    def hop(i, carry):
        source = count - 1 - i
        same = seg_ref[source * rows] == seg_ref[jnp.minimum((source + 1) * rows, last)]
        linked = jnp.where(same, 1.0, 0.0)
        carry_scr[...] = heads_ref[source - place] + linked * through_scr[...] * carry_scr[...]
        return carry

    lax.fori_loop(0, count - 1 - place, hop, 0)

    def step(i, state):
        values, sums = state
        t = rows - 1 - i
        link = link_at(seg_ref, start + t)
        grad = grad_scr[pl.ds(t, subs, stride=rows), :]
        inputs = input_scr[pl.ds(t, subs, stride=rows), :]
        values = tuple(grad + decay_scr[link, m] * values[m] for m in range(modes))
        sums = tuple(sums[m] + inputs * values[m] for m in range(modes))
        parts = [residue_scr[m] * values[m] for m in range(modes)]
        while len(parts) > 1:
            parts = [a + b for a, b in zip(parts[::2], parts[1::2])]
        conv_scr[pl.ds(t, subs, stride=rows), :] = parts[0]
        return values, sums

    zero = jnp.zeros((subs, LANES), jnp.float32)
    values = tuple(carry_scr[m] for m in range(modes))
    _, sums = lax.fori_loop(0, rows, step, (values, (zero,) * modes), unroll=4)
    for m in range(modes):
        mode_scr[pl.ds(m, subs, stride=modes), :] = sums[m]
    fold(mode_scr, filter_ref, lambda v: v)
    fold(conv_scr, conv_ref, lambda v: v.astype(conv_ref.dtype))


def exchange_kernel(head_ref, out_ref, send_sem, recv_sem):
    count = out_ref.shape[0]
    place = lax.axis_index("ctx")
    out_ref[...] = jnp.zeros_like(out_ref)
    barrier = pltpu.get_barrier_semaphore()
    for d in range(1, count):
        other = lax.rem(place + d, count)
        pl.semaphore_signal(barrier, inc=1, device_id={"ctx": other}, device_id_type=MESH)
    pl.semaphore_wait(barrier, count - 1)
    copies = []
    for d in range(1, count):
        other = jnp.maximum(place - d, 0)
        copies.append(pltpu.make_async_remote_copy(
            src_ref=head_ref,
            dst_ref=out_ref.at[d],
            send_sem=send_sem.at[d],
            recv_sem=recv_sem.at[d],
            device_id={"ctx": other},
            device_id_type=MESH,
        ))
    for d in range(1, count):
        pl.when(place >= d)(copies[d - 1].start)
    for d in range(1, count):
        pl.when(place >= d)(copies[d - 1].wait_send)
        pl.when(place + d < count)(copies[d - 1].wait_recv)


def fused_kernel(
    seg_ref, grad_hbm, input_hbm, residue_hbm, rate_hbm, w_ref, out_ref, filter_ref,
    grad_ref, input_ref, residue_ref, rate_ref, conv_ref, part_ref, head_ref, heads_ref,
    grad_scr, input_scr, conv_scr, mode_scr, through_scr, decay_scr, residue_scr, carry_scr,
    blocks, weights, total, parts,
    send_sem, recv_sem, weight_sem, part_send, part_recv, head_send, head_recv, load_sem,
):
    rows, width = conv_ref.shape
    modes = rate_ref.shape[0]
    subs = width // LANES
    part = rows // 4
    half = 2 * part
    count = parts.shape[0]
    place = lax.axis_index("ctx")
    me = lax.axis_index("head")
    core = lax.rem(me, 2)
    east = lax.rem(me // 2, 2)
    north = me // 4
    steps = {1: 1 - 2 * core, 2: 2 - 4 * east, 4: 4 - 8 * north}

    def apart(k):
        return me + sum(steps[bit] for bit in steps if k & bit)

    operands = []
    for i, (src, dst) in enumerate((
        (grad_hbm, grad_ref), (rate_hbm, rate_ref),
        (input_hbm, input_ref), (residue_hbm, residue_ref),
    )):
        operands.append(pltpu.make_async_copy(src, dst, load_sem.at[i]))
        operands[i].start()
    loads = []
    for k in range(8):
        loads.append(pltpu.make_async_copy(
            w_ref.at[:, pl.ds(pl.multiple_of(apart(k) * width, LANES), width)],
            weights.at[k],
            weight_sem.at[k],
        ))
        loads[k].start()

    barrier = pltpu.get_barrier_semaphore()
    for bit in steps:
        pl.semaphore_signal(barrier, inc=1, device_id={"head": apart(bit)}, device_id_type=MESH)
    for d in range(1, count):
        other = lax.rem(place + d, count)
        pl.semaphore_signal(barrier, inc=1, device_id={"ctx": other}, device_id_type=MESH)

    start = place * rows
    zero = jnp.zeros((subs, LANES), jnp.float32)
    operands[0].wait()
    spread(grad_ref, grad_scr, wide)
    operands[1].wait()
    fill_decay(rate_ref, mode_scr, decay_scr)

    def head_step(i, state):
        t = rows - 1 - i
        link = link_at(seg_ref, start + t)
        grad = grad_scr[pl.ds(t, subs, stride=rows), :]
        return tuple(grad + decay_scr[link, m] * state[m] for m in range(modes))

    state = lax.fori_loop(0, rows, head_step, (zero,) * modes, unroll=8)
    for m in range(modes):
        mode_scr[pl.ds(m * subs, subs), :] = state[m]
    head_ref[...] = mode_scr[...].astype(head_ref.dtype)
    pl.semaphore_wait(barrier, 3 + count - 1)
    copies = []
    for d in range(1, count):
        copies.append(pltpu.make_async_remote_copy(
            src_ref=head_ref,
            dst_ref=heads_ref.at[d],
            send_sem=head_send.at[d],
            recv_sem=head_recv.at[d],
            device_id={"ctx": jnp.maximum(place - d, 0)},
            device_id_type=MESH,
        ))
    for d in range(1, count):
        pl.when(place >= d)(copies[d - 1].start)

    spread(rate_ref, mode_scr, lambda v: jnp.exp(-rows * v))
    for m in range(modes):
        through_scr[pl.ds(m * subs, subs), :] = mode_scr[pl.ds(m, subs, stride=modes), :]
    operands[2].wait()
    spread(input_ref, input_scr, wide)
    operands[3].wait()
    spread(residue_ref, mode_scr, lambda v: v)
    for m in range(modes):
        residue_scr[m] = mode_scr[pl.ds(m, subs, stride=modes), :]
    carry_scr[...] = jnp.zeros_like(carry_scr)
    last = seg_ref.shape[0] - 1

    def hop(d):
        copies[d - 1].wait_recv()
        source = place + d
        same = seg_ref[source * rows] == seg_ref[jnp.minimum((source + 1) * rows, last)]
        linked = jnp.where(same, 1.0, 0.0)
        carry_scr[...] = wide(heads_ref[d]) + linked * through_scr[...] * carry_scr[...]

    for d in range(count - 1, 0, -1):
        pl.when(place + d < count)(functools.partial(hop, d))

    def step(i, state):
        values, sums = state
        t = rows - 1 - i
        link = link_at(seg_ref, start + t)
        grad = grad_scr[pl.ds(t, subs, stride=rows), :]
        inputs = input_scr[pl.ds(t, subs, stride=rows), :]
        values = tuple(grad + decay_scr[link, m] * values[m] for m in range(modes))
        sums = tuple(sums[m] + inputs * values[m] for m in range(modes))
        terms = [residue_scr[m] * values[m] for m in range(modes)]
        while len(terms) > 1:
            terms = [a + b for a, b in zip(terms[::2], terms[1::2])]
        conv_scr[pl.ds(t, subs, stride=rows), :] = terms[0]
        return values, sums

    def round_rows(first):
        for tile in range(subs):
            conv_ref[pl.ds(first, part), pl.ds(tile * LANES, LANES)] = conv_scr[
                pl.ds(tile * rows + first, part), :
            ].astype(conv_ref.dtype)

    def piece(k, h):
        if k == 0:
            return conv_ref.at[pl.ds(h * part, part)]
        return blocks.at[k - 1, pl.ds(h * part, part)]

    sent = {}

    def send(k, h, bit):
        copy = pltpu.make_async_remote_copy(
            src_ref=piece(k, h),
            dst_ref=piece(k ^ bit, h),
            send_sem=send_sem.at[(k ^ bit) - 1, h],
            recv_sem=recv_sem.at[(k ^ bit) - 1, h],
            device_id={"head": apart(bit)},
            device_id_type=MESH,
        )
        copy.start()
        sent[k ^ bit, h] = copy

    def multiply(k, first, size):
        def tile(n, carry):
            columns = pl.ds(pl.multiple_of(n * 256, 256), 256)
            source = conv_ref if k == 0 else blocks.at[k - 1]
            product = lax.dot_general(
                source[pl.ds(first, size), :],
                weights[k, columns, :],
                (((1,), (1,)), ((), ())),
                preferred_element_type=jnp.float32,
            )
            if k == 0:
                total[pl.ds(first, size), columns] = product
            else:
                total[pl.ds(first, size), columns] += product
            return carry

        lax.fori_loop(0, total.shape[1] // 256, tile, 0)

    state = (
        tuple(carry_scr[pl.ds(m * subs, subs), :] for m in range(modes)),
        (zero,) * modes,
    )
    for h in (3, 2, 1, 0):
        done = (3 - h) * part
        state = lax.fori_loop(done, done + part, step, state, unroll=4)
        round_rows(h * part)
        send(0, h, 2)
        send(0, h, 4)
        send(0, h, 1)
    state = state[1]
    for m in range(modes):
        mode_scr[pl.ds(m, subs, stride=modes), :] = state[m]
    fold(mode_scr, part_ref, lambda v: v)
    sums = []
    for d in range(1, count):
        other = lax.rem(place + d, count)
        sums.append(pltpu.make_async_remote_copy(
            src_ref=part_ref,
            dst_ref=parts.at[count - d],
            send_sem=part_send.at[d],
            recv_sem=part_recv.at[count - d],
            device_id={"ctx": other},
            device_id_type=MESH,
        ))
        sums[-1].start()
    parts[0] = part_ref[...]
    loads[0].wait()
    multiply(0, 0, rows)
    for k in (1, 2, 3, 4, 5):
        loads[k].wait()

    def pass_on(h):
        sent[2, h].wait_recv()
        sent[4, h].wait_recv()
        if h % 2:
            send(2, h, 4)
        else:
            send(4, h, 2)
        send(2, h, 1)
        send(4, h, 1)

    def lower(k, first):
        for h in (1, 0):
            sent[k, first + h].wait_recv()
        multiply(k, first * part, half)

    pass_on(3)
    for h in (3, 2, 1, 0):
        sent[1, h].wait_recv()
    multiply(1, 0, rows)
    pass_on(2)
    multiply(2, half, half)
    multiply(4, half, half)
    lower(3, 2)
    lower(5, 2)
    for copy in sums:
        copy.wait()
    value = parts[lax.rem(count - place, count)]
    for z in range(1, count):
        value = value + parts[lax.rem(z + count - place, count)]
    filter_ref[...] = value
    pass_on(1)
    pass_on(0)
    multiply(2, 0, half)
    multiply(4, 0, half)
    lower(3, 0)
    lower(5, 0)
    loads[6].wait()
    loads[7].wait()
    for first in (2, 0):
        for h in (1, 0):
            sent[6, first + h].wait_recv()
            send(6, first + h, 1)
        multiply(6, first * part, half)
        lower(7, first)
    for d in range(1, count):
        pl.when(place >= d)(copies[d - 1].wait_send)
    for copy in sent.values():
        copy.wait_send()
    out_ref[...] = total[...].astype(out_ref.dtype)


def exchange(head):
    count = lax.axis_size("ctx")
    return pl.pallas_call(
        exchange_kernel,
        out_shape=jax.ShapeDtypeStruct((count,) + head.shape, head.dtype),
        in_specs=[VMEM],
        out_specs=VMEM,
        scratch_shapes=[pltpu.SemaphoreType.DMA((count,))] * 2,
        compiler_params=pltpu.CompilerParams(collective_id=1, has_side_effects=True),
        name="head_exchange",
    )(head)


def fused(out_grad, conv_input, residues, decay_rate, segments, w_in):
    rows, width = out_grad.shape
    modes = residues.shape[0]
    features = w_in.shape[0]
    subs = width // LANES
    count = lax.axis_size("ctx")
    dma = pltpu.SemaphoreType.DMA
    f32, bf16 = jnp.float32, jnp.bfloat16
    tall = pltpu.VMEM((rows * subs, LANES), f32)
    packed = pltpu.VMEM((modes, subs, LANES), f32)
    flat = pltpu.VMEM((modes * subs, LANES), f32)
    block = pltpu.VMEM((rows, width), bf16)
    small = pltpu.VMEM((modes, width), f32)
    return pl.pallas_call(
        fused_kernel,
        out_shape=(
            jax.ShapeDtypeStruct((rows, features), bf16),
            jax.ShapeDtypeStruct((modes, width), f32),
        ),
        in_specs=[SMEM] + [pl.BlockSpec(memory_space=pl.ANY)] * 5,
        out_specs=(VMEM, VMEM),
        scratch_shapes=[
            block, block, small, small, block, small,
            pltpu.VMEM((modes * subs, LANES), bf16),
            pltpu.VMEM((count, modes * subs, LANES), bf16),
            tall, tall, tall,
            flat, flat,
            pltpu.VMEM((2, modes, subs, LANES), f32),
            packed, flat,
            pltpu.VMEM((7, rows, width), bf16),
            pltpu.VMEM((8, features, width), bf16),
            pltpu.VMEM((rows, features), f32),
            pltpu.VMEM((count, modes, width), f32),
            dma((7, 4)), dma((7, 4)), dma((8,)), dma((count,)), dma((count,)),
            dma((count,)), dma((count,)), dma((4,)),
        ],
        compiler_params=pltpu.CompilerParams(
            collective_id=2, has_side_effects=True, vmem_limit_bytes=56 << 20
        ),
        cost_estimate=pl.CostEstimate(
            flops=16 * rows * width * features,
            bytes_accessed=16 * features * width,
            transcendentals=0,
        ),
        name="fused_backward",
    )(segments, out_grad, conv_input, residues, decay_rate, w_in)


def local(out_grad, conv_input, residues, decay_rate, segments, w_in):
    if lax.axis_size("head") == 8:
        return fused(out_grad, conv_input, residues, decay_rate, segments, w_in)
    rows, width = out_grad.shape
    modes = residues.shape[0]
    subs = width // LANES
    f32 = jnp.float32
    tall = pltpu.VMEM((rows * subs, LANES), f32)
    flat = pltpu.VMEM((modes * subs, LANES), f32)
    packed = pltpu.VMEM((modes, subs, LANES), f32)
    decays = pltpu.VMEM((2, modes, subs, LANES), f32)
    params = pltpu.CompilerParams(vmem_limit_bytes=32 << 20)
    head = pl.pallas_call(
        head_kernel,
        out_shape=jax.ShapeDtypeStruct((modes, subs, LANES), f32),
        in_specs=[SMEM, VMEM, VMEM],
        out_specs=VMEM,
        scratch_shapes=[tall, flat, decays],
        compiler_params=params,
        name="head_state",
    )(segments, out_grad, decay_rate)
    heads = exchange(head)
    conv_grad, partial = pl.pallas_call(
        main_kernel,
        out_shape=(
            jax.ShapeDtypeStruct((rows, width), jnp.bfloat16),
            jax.ShapeDtypeStruct((modes, width), f32),
        ),
        in_specs=[SMEM] + [VMEM] * 5,
        out_specs=(VMEM, VMEM),
        scratch_shapes=[tall, tall, tall, flat, packed, decays, packed, packed],
        compiler_params=params,
        name="adjoint_scan",
    )(segments, out_grad, conv_input, residues, decay_rate, heads)
    filter_grad = lax.psum(partial, "ctx")
    d_input = lax.dot_general(
        lax.all_gather(conv_grad, "head", axis=1, tiled=True),
        w_in,
        (((1,), (1,)), ((), ())),
        preferred_element_type=f32,
    )
    return (d_input.astype(jnp.bfloat16), filter_grad)


def solution(mesh):
    placed = (
        P("ctx", "head"),
        P("ctx", "head"),
        P(None, "head"),
        P(None, "head"),
        P(),
        P("head", None),
    )
    return jax.shard_map(
        local,
        mesh=mesh,
        in_specs=placed,
        out_specs=(P("ctx", "head"), P(None, "head")),
        check_vma=False,
    )
```

```python
import functools

import jax
import jax.numpy as jnp
from jax import lax
from jax.experimental import pallas as pl
from jax.experimental.pallas import tpu as pltpu
from jax.sharding import PartitionSpec as P

LANES = 128
VMEM = pl.BlockSpec(memory_space=pltpu.VMEM)
MESH = pl.DeviceIdType.MESH
SMEM = pl.BlockSpec(memory_space=pltpu.SMEM)


def spread(src, dst, convert):
    rows, width = src.shape
    tiles = width // LANES
    pitch = dst.shape[0] // tiles
    for tile in range(tiles):
        dst[pl.ds(tile * pitch, rows), :] = convert(src[:, pl.ds(tile * LANES, LANES)])


def fold(src, dst, convert):
    rows, width = dst.shape
    for tile in range(width // LANES):
        dst[:, pl.ds(tile * LANES, LANES)] = convert(src[pl.ds(tile * rows, rows), :])


def wide(value):
    return value.astype(jnp.float32)


def fill_decay(rate_ref, mode_scr, decay_scr):
    modes = rate_ref.shape[0]
    subs = rate_ref.shape[1] // LANES
    spread(rate_ref, mode_scr, lambda v: jnp.exp(-v))
    for m in range(modes):
        decay_scr[0, m] = jnp.zeros((subs, LANES), jnp.float32)
        decay_scr[1, m] = mode_scr[pl.ds(m, subs, stride=modes), :]


def link_at(seg_ref, token):
    last = seg_ref.shape[0] - 1
    same = seg_ref[token] == seg_ref[jnp.minimum(token + 1, last)]
    return jnp.where(same, 1, 0)


def head_kernel(seg_ref, grad_ref, rate_ref, out_ref, grad_scr, mode_scr, decay_scr):
    rows, width = grad_ref.shape
    modes = rate_ref.shape[0]
    subs = width // LANES
    start = lax.axis_index("ctx") * rows
    spread(grad_ref, grad_scr, wide)
    fill_decay(rate_ref, mode_scr, decay_scr)

    def step(i, state):
        t = rows - 1 - i
        link = link_at(seg_ref, start + t)
        grad = grad_scr[pl.ds(t, subs, stride=rows), :]
        return tuple(grad + decay_scr[link, m] * state[m] for m in range(modes))

    zero = jnp.zeros((subs, LANES), jnp.float32)
    state = lax.fori_loop(0, rows, step, (zero,) * modes, unroll=8)
    for m in range(modes):
        out_ref[m] = state[m]


def main_kernel(
    seg_ref, grad_ref, input_ref, residue_ref, rate_ref, heads_ref,
    conv_ref, filter_ref,
    grad_scr, input_scr, conv_scr, mode_scr, through_scr, decay_scr, residue_scr, carry_scr,
):
    rows, width = grad_ref.shape
    modes = rate_ref.shape[0]
    subs = width // LANES
    place = lax.axis_index("ctx")
    count = heads_ref.shape[0]
    start = place * rows
    spread(grad_ref, grad_scr, wide)
    spread(input_ref, input_scr, wide)
    spread(residue_ref, mode_scr, lambda v: v)
    for m in range(modes):
        residue_scr[m] = mode_scr[pl.ds(m, subs, stride=modes), :]
    spread(rate_ref, mode_scr, lambda v: jnp.exp(-rows * v))
    for m in range(modes):
        through_scr[m] = mode_scr[pl.ds(m, subs, stride=modes), :]
    fill_decay(rate_ref, mode_scr, decay_scr)
    carry_scr[...] = jnp.zeros_like(carry_scr)
    last = seg_ref.shape[0] - 1

    def hop(i, carry):
        source = count - 1 - i
        same = seg_ref[source * rows] == seg_ref[jnp.minimum((source + 1) * rows, last)]
        linked = jnp.where(same, 1.0, 0.0)
        carry_scr[...] = heads_ref[source - place] + linked * through_scr[...] * carry_scr[...]
        return carry

    lax.fori_loop(0, count - 1 - place, hop, 0)

    def step(i, state):
        values, sums = state
        t = rows - 1 - i
        link = link_at(seg_ref, start + t)
        grad = grad_scr[pl.ds(t, subs, stride=rows), :]
        inputs = input_scr[pl.ds(t, subs, stride=rows), :]
        values = tuple(grad + decay_scr[link, m] * values[m] for m in range(modes))
        sums = tuple(sums[m] + inputs * values[m] for m in range(modes))
        parts = [residue_scr[m] * values[m] for m in range(modes)]
        while len(parts) > 1:
            parts = [a + b for a, b in zip(parts[::2], parts[1::2])]
        conv_scr[pl.ds(t, subs, stride=rows), :] = parts[0]
        return values, sums

    zero = jnp.zeros((subs, LANES), jnp.float32)
    values = tuple(carry_scr[m] for m in range(modes))
    _, sums = lax.fori_loop(0, rows, step, (values, (zero,) * modes), unroll=4)
    for m in range(modes):
        mode_scr[pl.ds(m, subs, stride=modes), :] = sums[m]
    fold(mode_scr, filter_ref, lambda v: v)
    fold(conv_scr, conv_ref, lambda v: v.astype(conv_ref.dtype))


def exchange_kernel(head_ref, out_ref, send_sem, recv_sem):
    count = out_ref.shape[0]
    place = lax.axis_index("ctx")
    out_ref[...] = jnp.zeros_like(out_ref)
    barrier = pltpu.get_barrier_semaphore()
    for d in range(1, count):
        other = lax.rem(place + d, count)
        pl.semaphore_signal(barrier, inc=1, device_id={"ctx": other}, device_id_type=MESH)
    pl.semaphore_wait(barrier, count - 1)
    copies = []
    for d in range(1, count):
        other = jnp.maximum(place - d, 0)
        copies.append(pltpu.make_async_remote_copy(
            src_ref=head_ref,
            dst_ref=out_ref.at[d],
            send_sem=send_sem.at[d],
            recv_sem=recv_sem.at[d],
            device_id={"ctx": other},
            device_id_type=MESH,
        ))
    for d in range(1, count):
        pl.when(place >= d)(copies[d - 1].start)
    for d in range(1, count):
        pl.when(place >= d)(copies[d - 1].wait_send)
        pl.when(place + d < count)(copies[d - 1].wait_recv)


def fused_kernel(
    seg_ref, grad_hbm, input_hbm, residue_hbm, rate_hbm, w_ref, out_ref, filter_ref,
    grad_ref, input_ref, residue_ref, rate_ref, conv_ref, part_ref, head_ref, heads_ref,
    grad_scr, input_scr, conv_scr, mode_scr, through_scr, decay_scr, residue_scr, carry_scr,
    blocks, weights, total, parts,
    send_sem, recv_sem, weight_sem, part_send, part_recv, head_send, head_recv, load_sem,
):
    rows, width = conv_ref.shape
    modes = rate_ref.shape[0]
    subs = width // LANES
    part = rows // 4
    half = 2 * part
    pitch = grad_scr.shape[0] // subs
    count = parts.shape[0]
    place = lax.axis_index("ctx")
    me = lax.axis_index("head")
    core = lax.rem(me, 2)
    east = lax.rem(me // 2, 2)
    north = me // 4
    steps = {1: 1 - 2 * core, 2: 2 - 4 * east, 4: 4 - 8 * north}

    def apart(k):
        return me + sum(steps[bit] for bit in steps if k & bit)

    operands = []
    for i, (src, dst) in enumerate((
        (grad_hbm, grad_ref), (rate_hbm, rate_ref),
        (input_hbm, input_ref), (residue_hbm, residue_ref),
    )):
        operands.append(pltpu.make_async_copy(src, dst, load_sem.at[i]))
        operands[i].start()
    loads = []
    for k in range(8):
        loads.append(pltpu.make_async_copy(
            w_ref.at[:, pl.ds(pl.multiple_of(apart(k) * width, LANES), width)],
            weights.at[k],
            weight_sem.at[k],
        ))
        loads[k].start()

    barrier = pltpu.get_barrier_semaphore()
    for bit in steps:
        pl.semaphore_signal(barrier, inc=1, device_id={"head": apart(bit)}, device_id_type=MESH)
    for d in range(1, count):
        other = lax.rem(place + d, count)
        pl.semaphore_signal(barrier, inc=1, device_id={"ctx": other}, device_id_type=MESH)

    start = place * rows
    zero = jnp.zeros((subs, LANES), jnp.float32)
    operands[0].wait()
    spread(grad_ref, grad_scr, wide)
    operands[1].wait()
    fill_decay(rate_ref, mode_scr, decay_scr)

    def head_step(i, state):
        t = rows - 1 - i
        link = link_at(seg_ref, start + t)
        grad = grad_scr[pl.ds(t, subs, stride=pitch), :]
        return tuple(grad + decay_scr[link, m] * state[m] for m in range(modes))

    state = lax.fori_loop(0, rows, head_step, (zero,) * modes, unroll=8)
    for m in range(modes):
        mode_scr[pl.ds(m * subs, subs), :] = state[m]
    head_ref[...] = mode_scr[...].astype(head_ref.dtype)
    pl.semaphore_wait(barrier, 3 + count - 1)
    copies = []
    for d in range(1, count):
        copies.append(pltpu.make_async_remote_copy(
            src_ref=head_ref,
            dst_ref=heads_ref.at[d],
            send_sem=head_send.at[d],
            recv_sem=head_recv.at[d],
            device_id={"ctx": jnp.maximum(place - d, 0)},
            device_id_type=MESH,
        ))
    for d in range(1, count):
        pl.when(place >= d)(copies[d - 1].start)

    spread(rate_ref, mode_scr, lambda v: jnp.exp(-rows * v))
    for m in range(modes):
        through_scr[pl.ds(m * subs, subs), :] = mode_scr[pl.ds(m, subs, stride=modes), :]
    operands[2].wait()
    spread(input_ref, input_scr, wide)
    operands[3].wait()
    spread(residue_ref, mode_scr, lambda v: v)
    for m in range(modes):
        residue_scr[m] = mode_scr[pl.ds(m, subs, stride=modes), :]
    carry_scr[...] = jnp.zeros_like(carry_scr)
    last = seg_ref.shape[0] - 1

    def hop(d):
        copies[d - 1].wait_recv()
        source = place + d
        same = seg_ref[source * rows] == seg_ref[jnp.minimum((source + 1) * rows, last)]
        linked = jnp.where(same, 1.0, 0.0)
        carry_scr[...] = wide(heads_ref[d]) + linked * through_scr[...] * carry_scr[...]

    for d in range(count - 1, 0, -1):
        pl.when(place + d < count)(functools.partial(hop, d))

    def step(i, state):
        values, sums = state
        t = rows - 1 - i
        link = link_at(seg_ref, start + t)
        grad = grad_scr[pl.ds(t, subs, stride=pitch), :]
        inputs = input_scr[pl.ds(t, subs, stride=pitch), :]
        values = tuple(grad + decay_scr[link, m] * values[m] for m in range(modes))
        sums = tuple(sums[m] + inputs * values[m] for m in range(modes))
        terms = [residue_scr[m] * values[m] for m in range(modes)]
        while len(terms) > 1:
            terms = [a + b for a, b in zip(terms[::2], terms[1::2])]
        conv_scr[pl.ds(t, subs, stride=pitch), :] = terms[0]
        return values, sums

    def round_rows(first):
        for tile in range(subs):
            conv_ref[pl.ds(first, part), pl.ds(tile * LANES, LANES)] = conv_scr[
                pl.ds(tile * pitch + first, part), :
            ].astype(conv_ref.dtype)

    def piece(k, h):
        if k == 0:
            return conv_ref.at[pl.ds(h * part, part)]
        return blocks.at[k - 1, pl.ds(h * part, part)]

    sent = {}

    def send(k, h, bit):
        copy = pltpu.make_async_remote_copy(
            src_ref=piece(k, h),
            dst_ref=piece(k ^ bit, h),
            send_sem=send_sem.at[(k ^ bit) - 1, h],
            recv_sem=recv_sem.at[(k ^ bit) - 1, h],
            device_id={"head": apart(bit)},
            device_id_type=MESH,
        )
        copy.start()
        sent[k ^ bit, h] = copy

    def multiply(k, first, size):
        def tile(n, carry):
            columns = pl.ds(pl.multiple_of(n * 256, 256), 256)
            source = conv_ref if k == 0 else blocks.at[k - 1]
            product = lax.dot_general(
                source[pl.ds(first, size), :],
                weights[k, columns, :],
                (((1,), (1,)), ((), ())),
                preferred_element_type=jnp.float32,
            )
            if k == 0:
                total[pl.ds(first, size), columns] = product
            else:
                total[pl.ds(first, size), columns] += product
            return carry

        lax.fori_loop(0, total.shape[1] // 256, tile, 0)

    state = (
        tuple(carry_scr[pl.ds(m * subs, subs), :] for m in range(modes)),
        (zero,) * modes,
    )
    for h in (3, 2, 1, 0):
        done = (3 - h) * part
        state = lax.fori_loop(done, done + part, step, state, unroll=8)
        round_rows(h * part)
        send(0, h, 2)
        send(0, h, 4)
        send(0, h, 1)
    state = state[1]
    for m in range(modes):
        mode_scr[pl.ds(m, subs, stride=modes), :] = state[m]
    fold(mode_scr, part_ref, lambda v: v)
    sums = []
    for d in range(1, count):
        other = lax.rem(place + d, count)
        sums.append(pltpu.make_async_remote_copy(
            src_ref=part_ref,
            dst_ref=parts.at[count - d],
            send_sem=part_send.at[d],
            recv_sem=part_recv.at[count - d],
            device_id={"ctx": other},
            device_id_type=MESH,
        ))
        sums[-1].start()
    parts[0] = part_ref[...]
    loads[0].wait()
    multiply(0, 0, rows)
    for k in (1, 2, 3, 4, 5):
        loads[k].wait()

    def pass_on(h):
        sent[2, h].wait_recv()
        sent[4, h].wait_recv()
        if h % 2:
            send(2, h, 4)
        else:
            send(4, h, 2)
        send(2, h, 1)
        send(4, h, 1)

    def lower(k, first):
        for h in (1, 0):
            sent[k, first + h].wait_recv()
        multiply(k, first * part, half)

    pass_on(3)
    for h in (3, 2, 1, 0):
        sent[1, h].wait_recv()
    multiply(1, 0, rows)
    pass_on(2)
    multiply(2, half, half)
    multiply(4, half, half)
    lower(3, 2)
    lower(5, 2)
    for copy in sums:
        copy.wait()
    value = parts[lax.rem(count - place, count)]
    for z in range(1, count):
        value = value + parts[lax.rem(z + count - place, count)]
    filter_ref[...] = value
    pass_on(1)
    pass_on(0)
    multiply(2, 0, half)
    multiply(4, 0, half)
    lower(3, 0)
    lower(5, 0)
    loads[6].wait()
    loads[7].wait()
    for first in (2, 0):
        for h in (1, 0):
            sent[6, first + h].wait_recv()
            send(6, first + h, 1)
        multiply(6, first * part, half)
        lower(7, first)
    for d in range(1, count):
        pl.when(place >= d)(copies[d - 1].wait_send)
    for copy in sent.values():
        copy.wait_send()
    out_ref[...] = total[...].astype(out_ref.dtype)


def exchange(head):
    count = lax.axis_size("ctx")
    return pl.pallas_call(
        exchange_kernel,
        out_shape=jax.ShapeDtypeStruct((count,) + head.shape, head.dtype),
        in_specs=[VMEM],
        out_specs=VMEM,
        scratch_shapes=[pltpu.SemaphoreType.DMA((count,))] * 2,
        compiler_params=pltpu.CompilerParams(collective_id=1, has_side_effects=True),
        name="head_exchange",
    )(head)


def fused(out_grad, conv_input, residues, decay_rate, segments, w_in):
    rows, width = out_grad.shape
    modes = residues.shape[0]
    features = w_in.shape[0]
    subs = width // LANES
    count = lax.axis_size("ctx")
    dma = pltpu.SemaphoreType.DMA
    f32, bf16 = jnp.float32, jnp.bfloat16
    tall = pltpu.VMEM(((rows + 8) * subs, LANES), f32)
    packed = pltpu.VMEM((modes, subs, LANES), f32)
    flat = pltpu.VMEM((modes * subs, LANES), f32)
    block = pltpu.VMEM((rows, width), bf16)
    small = pltpu.VMEM((modes, width), f32)
    return pl.pallas_call(
        fused_kernel,
        out_shape=(
            jax.ShapeDtypeStruct((rows, features), bf16),
            jax.ShapeDtypeStruct((modes, width), f32),
        ),
        in_specs=[SMEM] + [pl.BlockSpec(memory_space=pl.ANY)] * 5,
        out_specs=(VMEM, VMEM),
        scratch_shapes=[
            block, block, small, small, block, small,
            flat,
            pltpu.VMEM((count, modes * subs, LANES), f32),
            tall, tall, tall,
            flat, flat,
            pltpu.VMEM((2, modes, subs, LANES), f32),
            packed, flat,
            pltpu.VMEM((7, rows, width), bf16),
            pltpu.VMEM((8, features, width), bf16),
            pltpu.VMEM((rows, features), f32),
            pltpu.VMEM((count, modes, width), f32),
            dma((7, 4)), dma((7, 4)), dma((8,)), dma((count,)), dma((count,)),
            dma((count,)), dma((count,)), dma((4,)),
        ],
        compiler_params=pltpu.CompilerParams(
            collective_id=2, has_side_effects=True, vmem_limit_bytes=56 << 20
        ),
        cost_estimate=pl.CostEstimate(
            flops=16 * rows * width * features,
            bytes_accessed=16 * features * width,
            transcendentals=0,
        ),
        name="fused_backward",
    )(segments, out_grad, conv_input, residues, decay_rate, w_in)


def local(out_grad, conv_input, residues, decay_rate, segments, w_in):
    if lax.axis_size("head") == 8:
        return fused(out_grad, conv_input, residues, decay_rate, segments, w_in)
    rows, width = out_grad.shape
    modes = residues.shape[0]
    subs = width // LANES
    f32 = jnp.float32
    tall = pltpu.VMEM((rows * subs, LANES), f32)
    flat = pltpu.VMEM((modes * subs, LANES), f32)
    packed = pltpu.VMEM((modes, subs, LANES), f32)
    decays = pltpu.VMEM((2, modes, subs, LANES), f32)
    params = pltpu.CompilerParams(vmem_limit_bytes=32 << 20)
    head = pl.pallas_call(
        head_kernel,
        out_shape=jax.ShapeDtypeStruct((modes, subs, LANES), f32),
        in_specs=[SMEM, VMEM, VMEM],
        out_specs=VMEM,
        scratch_shapes=[tall, flat, decays],
        compiler_params=params,
        name="head_state",
    )(segments, out_grad, decay_rate)
    heads = exchange(head)
    conv_grad, partial = pl.pallas_call(
        main_kernel,
        out_shape=(
            jax.ShapeDtypeStruct((rows, width), jnp.bfloat16),
            jax.ShapeDtypeStruct((modes, width), f32),
        ),
        in_specs=[SMEM] + [VMEM] * 5,
        out_specs=(VMEM, VMEM),
        scratch_shapes=[tall, tall, tall, flat, packed, decays, packed, packed],
        compiler_params=params,
        name="adjoint_scan",
    )(segments, out_grad, conv_input, residues, decay_rate, heads)
    filter_grad = lax.psum(partial, "ctx")
    d_input = lax.dot_general(
        lax.all_gather(conv_grad, "head", axis=1, tiled=True),
        w_in,
        (((1,), (1,)), ((), ())),
        preferred_element_type=f32,
    )
    return (d_input.astype(jnp.bfloat16), filter_grad)


def solution(mesh):
    placed = (
        P("ctx", "head"),
        P("ctx", "head"),
        P(None, "head"),
        P(None, "head"),
        P(),
        P("head", None),
    )
    return jax.shard_map(
        local,
        mesh=mesh,
        in_specs=placed,
        out_specs=(P("ctx", "head"), P(None, "head")),
        check_vma=False,
    )
```

```python
import functools

import jax
import jax.numpy as jnp
from jax import lax
from jax.experimental import pallas as pl
from jax.experimental.pallas import tpu as pltpu
from jax.sharding import PartitionSpec as P

LANES = 128
VMEM = pl.BlockSpec(memory_space=pltpu.VMEM)
MESH = pl.DeviceIdType.MESH
SMEM = pl.BlockSpec(memory_space=pltpu.SMEM)


def spread(src, dst, convert):
    rows, width = src.shape
    tiles = width // LANES
    pitch = dst.shape[0] // tiles
    for tile in range(tiles):
        dst[pl.ds(tile * pitch, rows), :] = convert(src[:, pl.ds(tile * LANES, LANES)])


def fold(src, dst, convert):
    rows, width = dst.shape
    for tile in range(width // LANES):
        dst[:, pl.ds(tile * LANES, LANES)] = convert(src[pl.ds(tile * rows, rows), :])


def wide(value):
    return value.astype(jnp.float32)


def fill_decay(rate_ref, mode_scr, decay_scr):
    modes = rate_ref.shape[0]
    subs = rate_ref.shape[1] // LANES
    spread(rate_ref, mode_scr, lambda v: jnp.exp(-v))
    for m in range(modes):
        decay_scr[0, m] = jnp.zeros((subs, LANES), jnp.float32)
        decay_scr[1, m] = mode_scr[pl.ds(m, subs, stride=modes), :]


def link_at(seg_ref, token):
    last = seg_ref.shape[0] - 1
    same = seg_ref[token] == seg_ref[jnp.minimum(token + 1, last)]
    return jnp.where(same, 1, 0)


def head_kernel(seg_ref, grad_ref, rate_ref, out_ref, grad_scr, mode_scr, decay_scr):
    rows, width = grad_ref.shape
    modes = rate_ref.shape[0]
    subs = width // LANES
    start = lax.axis_index("ctx") * rows
    spread(grad_ref, grad_scr, wide)
    fill_decay(rate_ref, mode_scr, decay_scr)

    def step(i, state):
        t = rows - 1 - i
        link = link_at(seg_ref, start + t)
        grad = grad_scr[pl.ds(t, subs, stride=rows), :]
        return tuple(grad + decay_scr[link, m] * state[m] for m in range(modes))

    zero = jnp.zeros((subs, LANES), jnp.float32)
    state = lax.fori_loop(0, rows, step, (zero,) * modes, unroll=8)
    for m in range(modes):
        out_ref[m] = state[m]


def main_kernel(
    seg_ref, grad_ref, input_ref, residue_ref, rate_ref, heads_ref,
    conv_ref, filter_ref,
    grad_scr, input_scr, conv_scr, mode_scr, through_scr, decay_scr, residue_scr, carry_scr,
):
    rows, width = grad_ref.shape
    modes = rate_ref.shape[0]
    subs = width // LANES
    place = lax.axis_index("ctx")
    count = heads_ref.shape[0]
    start = place * rows
    spread(grad_ref, grad_scr, wide)
    spread(input_ref, input_scr, wide)
    spread(residue_ref, mode_scr, lambda v: v)
    for m in range(modes):
        residue_scr[m] = mode_scr[pl.ds(m, subs, stride=modes), :]
    spread(rate_ref, mode_scr, lambda v: jnp.exp(-rows * v))
    for m in range(modes):
        through_scr[m] = mode_scr[pl.ds(m, subs, stride=modes), :]
    fill_decay(rate_ref, mode_scr, decay_scr)
    carry_scr[...] = jnp.zeros_like(carry_scr)
    last = seg_ref.shape[0] - 1

    def hop(i, carry):
        source = count - 1 - i
        same = seg_ref[source * rows] == seg_ref[jnp.minimum((source + 1) * rows, last)]
        linked = jnp.where(same, 1.0, 0.0)
        carry_scr[...] = heads_ref[source - place] + linked * through_scr[...] * carry_scr[...]
        return carry

    lax.fori_loop(0, count - 1 - place, hop, 0)

    def step(i, state):
        values, sums = state
        t = rows - 1 - i
        link = link_at(seg_ref, start + t)
        grad = grad_scr[pl.ds(t, subs, stride=rows), :]
        inputs = input_scr[pl.ds(t, subs, stride=rows), :]
        values = tuple(grad + decay_scr[link, m] * values[m] for m in range(modes))
        sums = tuple(sums[m] + inputs * values[m] for m in range(modes))
        parts = [residue_scr[m] * values[m] for m in range(modes)]
        while len(parts) > 1:
            parts = [a + b for a, b in zip(parts[::2], parts[1::2])]
        conv_scr[pl.ds(t, subs, stride=rows), :] = parts[0]
        return values, sums

    zero = jnp.zeros((subs, LANES), jnp.float32)
    values = tuple(carry_scr[m] for m in range(modes))
    _, sums = lax.fori_loop(0, rows, step, (values, (zero,) * modes), unroll=4)
    for m in range(modes):
        mode_scr[pl.ds(m, subs, stride=modes), :] = sums[m]
    fold(mode_scr, filter_ref, lambda v: v)
    fold(conv_scr, conv_ref, lambda v: v.astype(conv_ref.dtype))


def exchange_kernel(head_ref, out_ref, send_sem, recv_sem):
    count = out_ref.shape[0]
    place = lax.axis_index("ctx")
    out_ref[...] = jnp.zeros_like(out_ref)
    barrier = pltpu.get_barrier_semaphore()
    for d in range(1, count):
        other = lax.rem(place + d, count)
        pl.semaphore_signal(barrier, inc=1, device_id={"ctx": other}, device_id_type=MESH)
    pl.semaphore_wait(barrier, count - 1)
    copies = []
    for d in range(1, count):
        other = jnp.maximum(place - d, 0)
        copies.append(pltpu.make_async_remote_copy(
            src_ref=head_ref,
            dst_ref=out_ref.at[d],
            send_sem=send_sem.at[d],
            recv_sem=recv_sem.at[d],
            device_id={"ctx": other},
            device_id_type=MESH,
        ))
    for d in range(1, count):
        pl.when(place >= d)(copies[d - 1].start)
    for d in range(1, count):
        pl.when(place >= d)(copies[d - 1].wait_send)
        pl.when(place + d < count)(copies[d - 1].wait_recv)


def fused_kernel(
    seg_ref, grad_hbm, input_hbm, residue_hbm, rate_hbm, w_ref, total, filter_ref,
    grad_ref, input_ref, residue_ref, rate_ref, conv_ref, part_ref, head_ref, heads_ref,
    grad_scr, input_scr, conv_scr, mode_scr, through_scr, decay_scr, residue_scr, carry_scr,
    blocks, weights, parts,
    send_sem, recv_sem, weight_sem, part_send, part_recv, head_send, head_recv, load_sem,
):
    rows, width = conv_ref.shape
    modes = rate_ref.shape[0]
    subs = width // LANES
    part = rows // 4
    half = 2 * part
    pitch = grad_scr.shape[0] // subs
    count = parts.shape[0]
    place = lax.axis_index("ctx")
    me = lax.axis_index("head")
    core = lax.rem(me, 2)
    east = lax.rem(me // 2, 2)
    north = me // 4
    steps = {1: 1 - 2 * core, 2: 2 - 4 * east, 4: 4 - 8 * north}

    def apart(k):
        return me + sum(steps[bit] for bit in steps if k & bit)

    operands = []
    for i, (src, dst) in enumerate((
        (grad_hbm, grad_ref), (rate_hbm, rate_ref),
        (input_hbm, input_ref), (residue_hbm, residue_ref),
    )):
        operands.append(pltpu.make_async_copy(src, dst, load_sem.at[i]))
        operands[i].start()
    loads = []
    for k in range(8):
        loads.append(pltpu.make_async_copy(
            w_ref.at[:, pl.ds(pl.multiple_of(apart(k) * width, LANES), width)],
            weights.at[k],
            weight_sem.at[k],
        ))
        loads[k].start()

    barrier = pltpu.get_barrier_semaphore()
    for bit in steps:
        pl.semaphore_signal(barrier, inc=1, device_id={"head": apart(bit)}, device_id_type=MESH)
    for d in range(1, count):
        other = lax.rem(place + d, count)
        pl.semaphore_signal(barrier, inc=1, device_id={"ctx": other}, device_id_type=MESH)

    start = place * rows
    zero = jnp.zeros((subs, LANES), jnp.float32)
    operands[0].wait()
    spread(grad_ref, grad_scr, wide)
    operands[1].wait()
    fill_decay(rate_ref, mode_scr, decay_scr)

    def head_step(i, state):
        t = rows - 1 - i
        link = link_at(seg_ref, start + t)
        grad = grad_scr[pl.ds(t, subs, stride=pitch), :]
        return tuple(grad + decay_scr[link, m] * state[m] for m in range(modes))

    state = lax.fori_loop(0, rows, head_step, (zero,) * modes, unroll=8)
    for m in range(modes):
        mode_scr[pl.ds(m * subs, subs), :] = state[m]
    head_ref[...] = mode_scr[...].astype(head_ref.dtype)
    pl.semaphore_wait(barrier, 3 + count - 1)
    copies = []
    for d in range(1, count):
        copies.append(pltpu.make_async_remote_copy(
            src_ref=head_ref,
            dst_ref=heads_ref.at[d],
            send_sem=head_send.at[d],
            recv_sem=head_recv.at[d],
            device_id={"ctx": jnp.maximum(place - d, 0)},
            device_id_type=MESH,
        ))
    for d in range(1, count):
        pl.when(place >= d)(copies[d - 1].start)

    spread(rate_ref, mode_scr, lambda v: jnp.exp(-rows * v))
    for m in range(modes):
        through_scr[pl.ds(m * subs, subs), :] = mode_scr[pl.ds(m, subs, stride=modes), :]
    operands[2].wait()
    spread(input_ref, input_scr, wide)
    operands[3].wait()
    spread(residue_ref, mode_scr, lambda v: v)
    for m in range(modes):
        residue_scr[m] = mode_scr[pl.ds(m, subs, stride=modes), :]
    carry_scr[...] = jnp.zeros_like(carry_scr)
    last = seg_ref.shape[0] - 1

    def hop(d):
        copies[d - 1].wait_recv()
        source = place + d
        same = seg_ref[source * rows] == seg_ref[jnp.minimum((source + 1) * rows, last)]
        linked = jnp.where(same, 1.0, 0.0)
        carry_scr[...] = wide(heads_ref[d]) + linked * through_scr[...] * carry_scr[...]

    for d in range(count - 1, 0, -1):
        pl.when(place + d < count)(functools.partial(hop, d))

    def step(i, state):
        values, sums = state
        t = rows - 1 - i
        link = link_at(seg_ref, start + t)
        grad = grad_scr[pl.ds(t, subs, stride=pitch), :]
        inputs = input_scr[pl.ds(t, subs, stride=pitch), :]
        values = tuple(grad + decay_scr[link, m] * values[m] for m in range(modes))
        sums = tuple(sums[m] + inputs * values[m] for m in range(modes))
        terms = [residue_scr[m] * values[m] for m in range(modes)]
        while len(terms) > 1:
            terms = [a + b for a, b in zip(terms[::2], terms[1::2])]
        conv_scr[pl.ds(t, subs, stride=pitch), :] = terms[0]
        return values, sums

    def round_rows(first):
        for tile in range(subs):
            conv_ref[pl.ds(first, part), pl.ds(tile * LANES, LANES)] = conv_scr[
                pl.ds(tile * pitch + first, part), :
            ].astype(conv_ref.dtype)

    def piece(k, h):
        if k == 0:
            return conv_ref.at[pl.ds(h * part, part)]
        return blocks.at[k - 1, pl.ds(h * part, part)]

    sent = {}

    def send(k, h, bit):
        copy = pltpu.make_async_remote_copy(
            src_ref=piece(k, h),
            dst_ref=piece(k ^ bit, h),
            send_sem=send_sem.at[(k ^ bit) - 1, h],
            recv_sem=recv_sem.at[(k ^ bit) - 1, h],
            device_id={"head": apart(bit)},
            device_id_type=MESH,
        )
        copy.start()
        sent[k ^ bit, h] = copy

    def multiply(k, first, size):
        def tile(n, carry):
            columns = pl.ds(pl.multiple_of(n * 256, 256), 256)
            source = conv_ref if k == 0 else blocks.at[k - 1]
            product = lax.dot_general(
                source[pl.ds(first, size), :],
                weights[k, columns, :],
                (((1,), (1,)), ((), ())),
                preferred_element_type=jnp.float32,
            )
            if k == 0:
                total[pl.ds(first, size), columns] = product
            else:
                total[pl.ds(first, size), columns] += product
            return carry

        lax.fori_loop(0, total.shape[1] // 256, tile, 0)

    state = (
        tuple(carry_scr[pl.ds(m * subs, subs), :] for m in range(modes)),
        (zero,) * modes,
    )
    for h in (3, 2, 1, 0):
        done = (3 - h) * part
        state = lax.fori_loop(done, done + part, step, state, unroll=8)
        round_rows(h * part)
        send(0, h, 2)
        send(0, h, 4)
        send(0, h, 1)
    state = state[1]
    for m in range(modes):
        mode_scr[pl.ds(m, subs, stride=modes), :] = state[m]
    fold(mode_scr, part_ref, lambda v: v)
    sums = []
    for d in range(1, count):
        other = lax.rem(place + d, count)
        sums.append(pltpu.make_async_remote_copy(
            src_ref=part_ref,
            dst_ref=parts.at[count - d],
            send_sem=part_send.at[d],
            recv_sem=part_recv.at[count - d],
            device_id={"ctx": other},
            device_id_type=MESH,
        ))
        sums[-1].start()
    parts[0] = part_ref[...]
    loads[0].wait()
    multiply(0, 0, rows)
    for k in (1, 2, 3, 4, 5):
        loads[k].wait()

    def pass_on(h):
        sent[2, h].wait_recv()
        sent[4, h].wait_recv()
        if h % 2:
            send(2, h, 4)
        else:
            send(4, h, 2)
        send(2, h, 1)
        send(4, h, 1)

    def lower(k, first):
        for h in (1, 0):
            sent[k, first + h].wait_recv()
        multiply(k, first * part, half)

    pass_on(3)
    for h in (3, 2, 1, 0):
        sent[1, h].wait_recv()
    multiply(1, 0, rows)
    pass_on(2)
    multiply(2, half, half)
    multiply(4, half, half)
    lower(3, 2)
    lower(5, 2)
    for copy in sums:
        copy.wait()
    for i, places in enumerate((range(count // 2), range(count // 2, count))):
        value = jnp.zeros((modes, width), jnp.float32)
        for z in places:
            value = value + parts[lax.rem(z + count - place, count)]
        filter_ref[i] = value
    pass_on(1)
    pass_on(0)
    multiply(2, 0, half)
    multiply(4, 0, half)
    lower(3, 0)
    lower(5, 0)
    loads[6].wait()
    loads[7].wait()
    for first in (2, 0):
        for h in (1, 0):
            sent[6, first + h].wait_recv()
            send(6, first + h, 1)
        multiply(6, first * part, half)
        lower(7, first)
    for d in range(1, count):
        pl.when(place >= d)(copies[d - 1].wait_send)
    for copy in sent.values():
        copy.wait_send()


def exchange(head):
    count = lax.axis_size("ctx")
    return pl.pallas_call(
        exchange_kernel,
        out_shape=jax.ShapeDtypeStruct((count,) + head.shape, head.dtype),
        in_specs=[VMEM],
        out_specs=VMEM,
        scratch_shapes=[pltpu.SemaphoreType.DMA((count,))] * 2,
        compiler_params=pltpu.CompilerParams(collective_id=1, has_side_effects=True),
        name="head_exchange",
    )(head)


def fused(out_grad, conv_input, residues, decay_rate, segments, w_in):
    rows, width = out_grad.shape
    modes = residues.shape[0]
    features = w_in.shape[0]
    subs = width // LANES
    count = lax.axis_size("ctx")
    dma = pltpu.SemaphoreType.DMA
    f32, bf16 = jnp.float32, jnp.bfloat16
    tall = pltpu.VMEM(((rows + 8) * subs, LANES), f32)
    packed = pltpu.VMEM((modes, subs, LANES), f32)
    flat = pltpu.VMEM((modes * subs, LANES), f32)
    block = pltpu.VMEM((rows, width), bf16)
    small = pltpu.VMEM((modes, width), f32)
    return pl.pallas_call(
        fused_kernel,
        out_shape=(
            jax.ShapeDtypeStruct((rows, features), f32),
            jax.ShapeDtypeStruct((2, modes, width), f32),
        ),
        in_specs=[SMEM] + [pl.BlockSpec(memory_space=pl.ANY)] * 5,
        out_specs=(VMEM, VMEM),
        scratch_shapes=[
            block, block, small, small, block, small,
            flat,
            pltpu.VMEM((count, modes * subs, LANES), f32),
            tall, tall, tall,
            flat, flat,
            pltpu.VMEM((2, modes, subs, LANES), f32),
            packed, flat,
            pltpu.VMEM((7, rows, width), bf16),
            pltpu.VMEM((8, features, width), bf16),
            pltpu.VMEM((count, modes, width), f32),
            dma((7, 4)), dma((7, 4)), dma((8,)), dma((count,)), dma((count,)),
            dma((count,)), dma((count,)), dma((4,)),
        ],
        compiler_params=pltpu.CompilerParams(
            collective_id=2, has_side_effects=True, vmem_limit_bytes=56 << 20
        ),
        cost_estimate=pl.CostEstimate(
            flops=16 * rows * width * features,
            bytes_accessed=16 * features * width,
            transcendentals=0,
        ),
        name="fused_backward",
    )(segments, out_grad, conv_input, residues, decay_rate, w_in)


def local(out_grad, conv_input, residues, decay_rate, segments, w_in):
    if lax.axis_size("head") == 8:
        total, halves = fused(out_grad, conv_input, residues, decay_rate, segments, w_in)
        return total.astype(jnp.bfloat16), halves[0] + halves[1]
    rows, width = out_grad.shape
    modes = residues.shape[0]
    subs = width // LANES
    f32 = jnp.float32
    tall = pltpu.VMEM((rows * subs, LANES), f32)
    flat = pltpu.VMEM((modes * subs, LANES), f32)
    packed = pltpu.VMEM((modes, subs, LANES), f32)
    decays = pltpu.VMEM((2, modes, subs, LANES), f32)
    params = pltpu.CompilerParams(vmem_limit_bytes=32 << 20)
    head = pl.pallas_call(
        head_kernel,
        out_shape=jax.ShapeDtypeStruct((modes, subs, LANES), f32),
        in_specs=[SMEM, VMEM, VMEM],
        out_specs=VMEM,
        scratch_shapes=[tall, flat, decays],
        compiler_params=params,
        name="head_state",
    )(segments, out_grad, decay_rate)
    heads = exchange(head)
    conv_grad, partial = pl.pallas_call(
        main_kernel,
        out_shape=(
            jax.ShapeDtypeStruct((rows, width), jnp.bfloat16),
            jax.ShapeDtypeStruct((modes, width), f32),
        ),
        in_specs=[SMEM] + [VMEM] * 5,
        out_specs=(VMEM, VMEM),
        scratch_shapes=[tall, tall, tall, flat, packed, decays, packed, packed],
        compiler_params=params,
        name="adjoint_scan",
    )(segments, out_grad, conv_input, residues, decay_rate, heads)
    filter_grad = lax.psum(partial, "ctx")
    d_input = lax.dot_general(
        lax.all_gather(conv_grad, "head", axis=1, tiled=True),
        w_in,
        (((1,), (1,)), ((), ())),
        preferred_element_type=f32,
    )
    return (d_input.astype(jnp.bfloat16), filter_grad)


def solution(mesh):
    placed = (
        P("ctx", "head"),
        P("ctx", "head"),
        P(None, "head"),
        P(None, "head"),
        P(),
        P("head", None),
    )
    return jax.shard_map(
        local,
        mesh=mesh,
        in_specs=placed,
        out_specs=(P("ctx", "head"), P(None, "head")),
        check_vma=False,
    )
```
